256 devices in a mesh: gx: 8 (over x, core), gy: 32 (over z, y).
Axes of the slice: x: 4, y: 4, z: 8, core: 2. Of those that a mesh axis runs over, the one named last changes fastest.
Arguments:
- source: float32 [128, 512, 256], P('gx', 'gy'), may hold values from -8 to 8
- conductivity: float32 [128, 512, 256], P('gx', 'gy'), may hold values from 1 to 10
- guess: float32 [128, 512, 256], P('gx', 'gy'), may hold values from -6 to 6
Outputs:
- updated: float32 [128, 512, 256], P('gx', 'gy')
The draws below stay inside these ranges and needn't reach their ends.
All inputs are finite; a program needn't handle non-finite values.
Results may differ from the reference program's by a relative error of at most 0.0003.
Values sent between devices are 32-bit elements; how exact they have to be, the bound alone decides.
A program may use at most 128 MiB of HBM per device.

```python
import math
import jax
import jax.numpy as jnp

NZ = 256
LEVELS = 5
PRE_SWEEPS = 2
POST_SWEEPS = 2
BOTTOM_SWEEPS = 8
NX = 128
NY = 512


def wave_sum(key):
    keys = jax.random.split(key, 3)
    numbers = jax.random.randint(keys[0], (4, 3), 1, 3).astype(jnp.float32)
    phases = jax.random.uniform(keys[1], (4,), jnp.float32, 0.0, 2.0 * math.pi)
    heights = jax.random.normal(keys[2], (4,), jnp.float32)
    coord_x = (jnp.arange(NX, dtype=jnp.float32) / NX)[:, None, None]
    coord_y = (jnp.arange(NY, dtype=jnp.float32) / NY)[None, :, None]
    coord_z = (jnp.arange(NZ, dtype=jnp.float32) / NZ)[None, None, :]
    total = jnp.zeros((NX, NY, NZ), jnp.float32)
    for index in range(4):
        angle_x = 2.0 * math.pi * numbers[index, 0] * coord_x
        angle_y = 2.0 * math.pi * numbers[index, 1] * coord_y
        angle_z = 2.0 * math.pi * numbers[index, 2] * coord_z
        total = total + heights[index] * jnp.sin(angle_x + angle_y + angle_z + phases[index])
    return total


def block_pattern(key, lowest, highest):
    heights = jax.random.uniform(key, (NX // 8, NY // 8, NZ // 8), jnp.float32, lowest, highest)
    index_x = jnp.arange(NX // 8, dtype=jnp.int32)[:, None, None]
    index_y = jnp.arange(NY // 8, dtype=jnp.int32)[None, :, None]
    index_z = jnp.arange(NZ // 8, dtype=jnp.int32)[None, None, :]
    parity = (index_x + index_y + index_z) % 2
    signs = 1.0 - 2.0 * parity.astype(jnp.float32)
    blocks = heights * signs
    return jnp.repeat(jnp.repeat(jnp.repeat(blocks, 8, 0), 8, 1), 8, 2)


def draw_source(key, part):
    key = jax.random.fold_in(key, 11)
    wave_key, noise_key, offset_key, block_key = jax.random.split(key, 4)
    smooth = wave_sum(wave_key)
    rough = jax.random.normal(noise_key, (NX, NY, NZ), jnp.float32)
    offset = jax.random.uniform(offset_key, (), jnp.float32, 0.5, 1.0)
    pattern = block_pattern(block_key, 2.0, 3.0)
    return jnp.clip(smooth + rough + offset + pattern, -8.0, 8.0)


def levels(own_key, extent, cuts, low, high):
    def one(dim, parts):
        steps = jax.random.uniform(jax.random.fold_in(jax.random.fold_in(own_key, 6), dim), (parts,), jnp.float32, low / len(cuts), high / len(cuts))
        return jnp.repeat(jnp.exp(steps), extent[dim] // parts).reshape((-1,) + (1,) * (len(extent) - dim - 1))

    level = one(*cuts[0])
    for cut in cuts[1:]:
        level = level * one(*cut)
    return level


def normal_values(own_key, extent, deviation, reach, shards=(), kind=jnp.bfloat16):
    loudness = levels(own_key, extent, shards, -0.22, 0.18) if shards else 1.0
    drawn = jax.random.normal(own_key, extent, jnp.float32) * deviation * loudness
    return jnp.minimum(jnp.maximum(drawn, -reach), reach).astype(kind)


def setup_inputs(seed: int = 0) -> dict:
    streams_of = jax.random.split(jax.random.key(seed), 4)
    source = draw_source(jax.random.fold_in(streams_of[3], 71), 0)
    conductivity = jnp.clip(jnp.exp(math.log(10.0) - 2.3025851 * jax.random.uniform(streams_of[1], (NX, NY, NZ), jnp.float32) ** levels(streams_of[1], (NX, NY, NZ), ((0, 8), (1, 32)), -0.2, 0.2)), 1.0, 10.0)
    guess = normal_values(streams_of[2], (NX, NY, NZ), 0.5, 6.0, ((0, 8), (1, 32)), jnp.float32)
    return dict(source=source, conductivity=conductivity, guess=guess)


OMEGA = 0.8


def harmonic(first, second):
    return 2.0 * first * second / (first + second)


def wrap_pad(values):
    return jnp.pad(values, ((1, 1), (1, 1), (0, 0)), mode="wrap")


def face_set(padded, factor):
    centre = padded[1:-1, 1:-1]
    east_x = harmonic(centre, padded[2:, 1:-1])
    west_x = harmonic(padded[:-2, 1:-1], centre)
    east_y = harmonic(centre, padded[1:-1, 2:])
    west_y = harmonic(padded[1:-1, :-2], centre)
    east_z = harmonic(centre, jnp.roll(centre, -1, 2))
    west_z = harmonic(jnp.roll(centre, 1, 2), centre)
    diagonal = ((east_x + west_x) + (east_y + west_y) + (east_z + west_z)) * factor
    return (east_x, west_x, east_y, west_y, east_z, west_z, diagonal, factor)


def operate(padded, coeffs):
    centre = padded[1:-1, 1:-1]
    total = coeffs[0] * (centre - padded[2:, 1:-1]) + coeffs[1] * (centre - padded[:-2, 1:-1])
    total = total + coeffs[2] * (centre - padded[1:-1, 2:]) + coeffs[3] * (centre - padded[1:-1, :-2])
    total = total + coeffs[4] * (centre - jnp.roll(centre, -1, 2)) + coeffs[5] * (centre - jnp.roll(centre, 1, 2))
    return total * coeffs[7]


def jacobi_step(field, padded, source, coeffs):
    return field + OMEGA * (source - operate(padded, coeffs)) / coeffs[6]


def restrict(values):
    first, second, third = values.shape
    return values.reshape(first // 2, 2, second // 2, 2, third // 2, 2).mean(axis=(1, 3, 5))


def prolong(values):
    return jnp.repeat(jnp.repeat(jnp.repeat(values, 2, 0), 2, 1), 2, 2)


def vcycle(grid_level, source, field, conductivity):
    if grid_level == LEVELS - 1:
        source = source - jnp.mean(source)
    coeffs = face_set(wrap_pad(conductivity), 0.25 ** grid_level)
    started = 0
    if field is None:
        field = OMEGA * source / coeffs[6]
        started = 1
    if grid_level == LEVELS - 1:
        for sweep_index in range(BOTTOM_SWEEPS - started):
            field = jacobi_step(field, wrap_pad(field), source, coeffs)
        return field
    for sweep_index in range(PRE_SWEEPS - started):
        field = jacobi_step(field, wrap_pad(field), source, coeffs)
    residual = source - operate(wrap_pad(field), coeffs)
    correction = vcycle(grid_level + 1, restrict(residual), None, restrict(conductivity))
    field = field + prolong(correction)
    for sweep_index in range(POST_SWEEPS):
        field = jacobi_step(field, wrap_pad(field), source, coeffs)
    return field


def reference(source, conductivity, guess):
    return vcycle(0, source, guess, conductivity)
```

```python
import jax
import jax.numpy as jnp
from jax import lax
from jax.experimental import pallas as pl
from jax.experimental.pallas import tpu as pltpu
from jax.sharding import PartitionSpec as P

MESH = pl.DeviceIdType.MESH
F32, BF16 = jnp.float32, jnp.bfloat16
OMEGA = 0.8
GX, GY, NYC, NZC = 8, 32, 4, 8
EIGHT = [(0, 1), (0, -1), (1, 1), (1, -1), (-1, 1), (-1, -1), (1, 0), (-1, 0)]


def harmonic(a, b):
    return 2.0 * a * b / (a + b)


def mm(a, m):
    hi = a.astype(BF16)
    lo = (a - hi.astype(F32)).astype(BF16)
    return jnp.dot(hi, m, preferred_element_type=F32) + jnp.dot(lo, m, preferred_element_type=F32)


def zp(s):
    if len(s) == 1:
        return (pltpu.roll(s[0], 127, 1),)
    last = lax.broadcasted_iota(jnp.int32, s[0].shape, 1) == 127
    a, b = pltpu.roll(s[0], 127, 1), pltpu.roll(s[1], 127, 1)
    return (jnp.where(last, b, a), jnp.where(last, a, b))


def zm(s):
    if len(s) == 1:
        return (pltpu.roll(s[0], 1, 1),)
    first = lax.broadcasted_iota(jnp.int32, s[0].shape, 1) == 0
    a, b = pltpu.roll(s[0], 1, 1), pltpu.roll(s[1], 1, 1)
    return (jnp.where(first, b, a), jnp.where(first, a, b))


def yp(s):
    return tuple(pltpu.roll(a, a.shape[0] - 1, 0) for a in s)


def ym(s):
    return tuple(pltpu.roll(a, 1, 0) for a in s)


def each(f, *slabs):
    return tuple(f(*a) for a in zip(*slabs))


def get(ref, x):
    if len(ref.shape) == 4:
        return (ref[x, 0], ref[x, 1])
    return (ref[x],)


def put(ref, x, s):
    if len(ref.shape) == 4:
        ref[x, 0] = s[0]
        ref[x, 1] = s[1]
    else:
        ref[x] = s[0]


def add(a, b):
    return each(lambda p, q: p + q, a, b)


def sub(a, b):
    return each(lambda p, q: p - q, a, b)


def mul(a, b):
    return each(lambda p, q: p * q, a, b)


def coefficients(c_ref, cx_ref, cy_ref, cz_ref, w_ref, slabs, unroll):
    c = get(c_ref, 0)
    n = get(c_ref, 1)
    first = each(harmonic, c, n)
    put(cx_ref, 0, first)

    def body(x, carry):
        c, before = carry
        n = get(c_ref, x + 1)
        ex = each(harmonic, c, n)
        ey = each(harmonic, c, yp(c))
        ez = each(harmonic, c, zp(c))
        d = add(add(add(ex, before), add(ey, ym(ey))), add(ez, zm(ez)))
        put(cx_ref, x, ex)
        put(cy_ref, x, ey)
        put(cz_ref, x, ez)
        put(w_ref, x, each(lambda p: OMEGA / p, d))
        return n, ex

    lax.fori_loop(1, slabs - 1, body, (n, first), unroll=unroll)


def flux_loop(v_ref, b_ref, cx_ref, cy_ref, cz_ref, lo, hi, emit, unroll):
    v = get(v_ref, lo)
    before = mul(get(cx_ref, lo - 1), sub(v, get(v_ref, lo - 1)))

    def body(x, carry):
        v, before = carry
        n = get(v_ref, x + 1)
        tx = mul(get(cx_ref, x), sub(n, v))
        ty = mul(get(cy_ref, x), sub(yp(v), v))
        tz = mul(get(cz_ref, x), sub(zp(v), v))
        r = add(add(sub(tx, before), sub(ty, ym(ty))), sub(tz, zm(tz)))
        emit(x, v, add(get(b_ref, x), r))
        return n, tx

    lax.fori_loop(lo, hi, body, (v, before), unroll=unroll)


def sweep(v_ref, to_ref, b_ref, cx_ref, cy_ref, cz_ref, w_ref, lo, hi, unroll):
    def emit(x, v, r):
        put(to_ref, x, add(v, mul(get(w_ref, x), r)))

    flux_loop(v_ref, b_ref, cx_ref, cy_ref, cz_ref, lo, hi, emit, unroll)


def lane(shape):
    return lax.broadcasted_iota(jnp.int32, shape, len(shape) - 1)


def three_zp(v):
    return jnp.where(lane(v.shape) % 32 == 31, pltpu.roll(v, 31, 2), pltpu.roll(v, 127, 2))


def three_zm(v):
    return jnp.where(lane(v.shape) % 32 == 0, pltpu.roll(v, 97, 2), pltpu.roll(v, 1, 2))


def three_xp(v):
    r = pltpu.roll(v, 64, 2)
    return jnp.where(lane(v.shape) < 64, r, pltpu.roll(r, GX - 1, 1))


def three_xm(v):
    r = pltpu.roll(v, 64, 2)
    return jnp.where(lane(v.shape) < 64, pltpu.roll(r, 1, 1), r)


def three_y(v):
    up, down = pltpu.roll(v, 96, 2), pltpu.roll(v, 32, 2)
    first = lane(v[1:-1].shape) % 64 < 32
    return (jnp.where(first, up[1:-1], down[2:]), jnp.where(first, up[:-2], down[1:-1]))


def four_zp(v):
    return pltpu.roll(v, 126, 2)


def four_zm(v):
    return pltpu.roll(v, 2, 2)


def four_xp(v):
    return pltpu.roll(v, GX - 1, 1)


def four_xm(v):
    return pltpu.roll(v, 1, 1)


def four_y(v):
    return v[2:], v[:-2]


THREE = (three_xp, three_xm, three_y, three_zp, three_zm)
FOUR = (four_xp, four_xm, four_y, four_zp, four_zm)
CH = 4


def wrap_rows(ref):
    ref[0] = ref[GY]
    ref[GY + 1] = ref[1]


def whole_coefficients(level, c_ref, k_ref):
    xp, xm, y, zplus, zminus = level

    def body(i, carry):
        g = i * CH
        ext = c_ref[pl.ds(g, CH + 2)]
        c = ext[1:-1]
        up, down = y(ext)
        ex = harmonic(c, xp(c))
        ez = harmonic(c, zplus(c))
        ey, wy = harmonic(c, up), harmonic(down, c)
        wx, wz = xm(ex), zminus(ez)
        d = (ex + wx) + (ey + wy) + (ez + wz)
        for j, value in enumerate((ex, wx, ey, wy, ez, wz, d, OMEGA / d)):
            k_ref[j, pl.ds(g, CH)] = value
        return carry

    lax.fori_loop(0, GY // CH, body, 0, unroll=True)


def whole_sum(level, v_ref, k_ref, emit):
    xp, xm, y, zplus, zminus = level

    def body(i, carry):
        g = i * CH
        ext = v_ref[pl.ds(g, CH + 2)]
        v = ext[1:-1]
        up, down = y(ext)
        k = [k_ref[j, pl.ds(g, CH)] for j in range(6)]
        s = (k[0] * xp(v) + k[1] * xm(v)) + (k[2] * up + k[3] * down)
        emit(g, v, s + (k[4] * zplus(v) + k[5] * zminus(v)))
        return carry

    lax.fori_loop(0, GY // CH, body, 0, unroll=True)


def whole_sweep(level, v_ref, to_ref, b_ref, k_ref):
    def emit(g, v, s):
        to_ref[pl.ds(g + 1, CH)] = (1.0 - OMEGA) * v + k_ref[7, pl.ds(g, CH)] * (b_ref[pl.ds(g + 1, CH)] + s)

    whole_sum(level, v_ref, k_ref, emit)
    wrap_rows(to_ref)


def coarsen_lanes(v):
    s = v + pltpu.roll(v, 64, 2)
    s = s + pltpu.roll(s, 32, 2)
    return s + jnp.where(lane(v.shape) % 2 == 0, pltpu.roll(s, 127, 2), pltpu.roll(s, 1, 2))


def kernel(
    src_ref, cond_ref, guess_ref, out_ref,
    V0, B0, C0, CX0, CY0, CZ0, W0, VA0, VB0, VH, TR, PE0, TP0,
    C1, CX1, CY1, CZ1, W1, B1, VA1, VB1, R1, TP1,
    C2, CX2, CY2, CZ2, W2, B2, VA2, VB2, R2, B2H, V2H,
    C3, B3, V3A, V3B, K3, C4, B4, V4A, V4B, K4,
    MR, M3, MP1, MP2, MP3,
    lsem, e0s, e0r, c1s, c1r, b1s, b1r, h0s, h0r, h2s, h2r, cas, car, cbs, cbr, bas, bar, bbs, bbr,
):
    gx, gy = lax.axis_index("gx"), lax.axis_index("gy")
    yc, zc = lax.rem(gy, NYC), lax.div(gy, NYC)

    def beside(dx, dy):
        return (lax.rem(gx + dx + GX, GX), lax.rem(gy + dy + GY, GY))

    def in_plane(k):
        return (lax.rem(gx + lax.div(k, NYC), GX), zc * NYC + lax.rem(yc + lax.rem(k, NYC), NYC))

    def along_z(k):
        return (gx, lax.rem(zc + k, NZC) * NYC + yc)

    def remote(src, dst, send, recv, device):
        return pltpu.make_async_remote_copy(
            src_ref=src, dst_ref=dst, send_sem=send, recv_sem=recv, device_id=device, device_id_type=MESH
        )

    loads = []
    for i, (ref, to) in enumerate(((cond_ref, C0), (guess_ref, V0), (src_ref, B0))):
        for h in range(2):
            loads.append(
                pltpu.make_async_copy(
                    ref.at[:, :, pl.ds(128 * h, 128)],
                    to.at[pl.ds(3, 16), h, pl.ds(4, 16), :],
                    lsem.at[2 * i + h],
                )
            )
    for copy in loads:
        copy.start()

    barrier = pltpu.get_barrier_semaphore()
    for dx, dy in EIGHT:
        pl.semaphore_signal(barrier, inc=1, device_id=beside(dx, dy), device_id_type=MESH)

    def greet_plane(k, carry):
        pl.semaphore_signal(barrier, inc=1, device_id=in_plane(k), device_id_type=MESH)
        return carry

    def greet_z(k, carry):
        pl.semaphore_signal(barrier, inc=1, device_id=along_z(k), device_id_type=MESH)
        return carry

    lax.fori_loop(1, GX * NYC, greet_plane, 0)
    lax.fori_loop(1, NZC, greet_z, 0)

    def matrix(rows, columns, rule):
        r = lax.broadcasted_iota(jnp.int32, (rows, columns), 0)
        c = lax.broadcasted_iota(jnp.int32, (rows, columns), 1)
        return jnp.where(rule(r, c), 1.0, 0.0).astype(BF16)

    MR[0:256] = matrix(256, 128, lambda r, c: r // 2 == c)
    MR[256:384] = matrix(128, 128, lambda r, c: r // 2 == c % 64)
    M3[...] = matrix(128, 128, lambda r, c: (r < 64) & (r // 2 == c % 32))
    MP1[...] = matrix(128, 256, lambda r, c: r == c // 2)
    MP2[...] = matrix(128, 128, lambda r, c: r == c // 2)
    MP3[...] = matrix(128, 512, lambda r, c: (r // 32 == c // 128) & (r % 32 == (c % 64) // 2))

    for copy in loads:
        copy.wait()
    pl.semaphore_wait(barrier, len(EIGHT) + GX * NYC - 1 + NZC - 1)

    def edge(base, extent, step, width):
        if step == 0:
            return base, base, extent
        if step == 1:
            return base + extent - width, base - width, width
        return base, base + extent, width

    def block_copy(ref, base, extent, step, width, send, recv):
        sx, tx, nx = edge(base[0], extent, step[0], width)
        sy, ty, ny = edge(base[1], extent, step[1], width)
        if len(ref.shape) == 4:
            src, dst = ref.at[pl.ds(sx, nx), :, pl.ds(sy, ny), :], ref.at[pl.ds(tx, nx), :, pl.ds(ty, ny), :]
        else:
            src, dst = ref.at[pl.ds(sx, nx), pl.ds(sy, ny), :], ref.at[pl.ds(tx, nx), pl.ds(ty, ny), :]
        return remote(src, dst, send, recv, beside(*step))

    def exchange(ref, base, extent, width, send, recv):
        return [block_copy(ref, base, extent, o, width, send.at[i], recv.at[i]) for i, o in enumerate(EIGHT)]

    e0c = exchange(C0, (3, 4), 16, 3, e0s.at[0], e0r.at[0])
    e0v = exchange(V0, (3, 4), 16, 3, e0s.at[1], e0r.at[1])
    e0b = exchange(B0, (3, 4), 16, 2, e0s.at[2], e0r.at[2])
    for copies in (e0c, e0v, e0b):
        for copy in copies:
            copy.start()

    def restrict_zero(ref, scale):
        pairs = [
            jnp.concatenate([ref[3 + 2 * k, h, 4:20] + ref[4 + 2 * k, h, 4:20] for h in range(2)], axis=1)
            for k in range(8)
        ]
        TR[0:8, 0:16] = mm(jnp.concatenate(pairs, axis=0), MR[0:256]).reshape(8, 16, 128)
        return (TR[0:8, pl.ds(0, 8, stride=2), :] + TR[0:8, pl.ds(1, 8, stride=2), :]) * scale

    def restrict_one(ref, x0, count, y0, rows, scale):
        pairs = [ref[x0 + 2 * k, y0 : y0 + rows] + ref[x0 + 1 + 2 * k, y0 : y0 + rows] for k in range(count)]
        TR[0:count, 0:rows] = mm(jnp.concatenate(pairs, axis=0), MR[256:384]).reshape(count, rows, 128)
        half = rows // 2
        return (TR[0:count, pl.ds(0, half, stride=2), :] + TR[0:count, pl.ds(1, half, stride=2), :]) * scale

    def restrict_two(ref, scale):
        pairs = jnp.concatenate([ref[4] + ref[5], ref[6] + ref[7]], axis=0)
        s = mm(pairs, M3[...]) * scale
        group = lax.broadcasted_iota(jnp.int32, (1, 128), 1) // 32
        row = jnp.zeros((1, 128), F32)
        for g in range(4):
            at = 16 * (g // 2) + 4 + 2 * (g % 2)
            row = jnp.where(group == g, s[at : at + 1] + s[at + 1 : at + 2], row)
        return row

    def plane_copy(ref, k, send, recv):
        part = ref.at[gy + 1, pl.ds(gx, 1), :]
        return remote(part, part, send.at[k], recv.at[k], in_plane(k))

    def z_copy(ref, k, send, recv):
        part = ref.at[pl.ds(zc * NYC + 1, NYC)]
        return remote(part, part, send.at[k], recv.at[k], along_z(k))

    def start_plane(ref, send, recv):
        def go(k, carry):
            plane_copy(ref, k, send, recv).start()
            return carry

        lax.fori_loop(1, GX * NYC, go, 0)

    def landed_plane(ref, send, recv):
        def go(k, carry):
            plane_copy(ref, k, send, recv).wait_recv()
            return carry

        lax.fori_loop(1, GX * NYC, go, 0)

    def start_z(ref, send, recv):
        for k in range(1, NZC):
            z_copy(ref, k, send, recv).start()

    def landed_z(ref, send, recv):
        for k in range(1, NZC):
            z_copy(ref, k, send, recv).wait_recv()

    def sent(ref, plane_send, plane_recv, z_send, z_recv):
        def go(k, carry):
            plane_copy(ref, k, plane_send, plane_recv).wait_send()
            return carry

        lax.fori_loop(1, GX * NYC, go, 0)
        for k in range(1, NZC):
            z_copy(ref, k, z_send, z_recv).wait_send()

    C1[8:16, 8:16] = restrict_zero(C0, 0.125 * 0.25)
    c1 = exchange(C1, (8, 8), 8, 8, c1s, c1r)
    for copy in c1:
        copy.start()
    C2[4:8, 4:8] = restrict_one(C1, 8, 4, 8, 8, 0.125 * 0.25)
    C3[gy + 1, pl.ds(gx, 1), :] = restrict_two(C2, 0.125 * 0.25)
    start_plane(C3, cas, car)

    for copy in e0c:
        copy.wait_recv()
    coefficients(C0, CX0, CY0, CZ0, W0, 22, 2)
    for copy in e0v + e0b:
        copy.wait_recv()
    zero = (B0, CX0, CY0, CZ0)
    sweep(V0, VA0, *zero, W0, 1, 21, 2)
    sweep(VA0, VB0, *zero, W0, 2, 20, 2)
    flux_loop(VB0, *zero, 3, 19, lambda x, v, r: put(VA0, x, r), 2)
    B1[8:16, 8:16] = restrict_zero(VA0, 0.125)
    b1 = exchange(B1, (8, 8), 8, 8, b1s, b1r)
    for copy in b1:
        copy.start()

    h0 = [
        remote(VB0.at[pl.ds(sx, nx), :, pl.ds(sy, ny), :], VH.at[pl.ds(tx, nx), :, pl.ds(ty, ny), :],
               h0s.at[i], h0r.at[i], beside(*o))
        for i, (o, (sx, tx, nx), (sy, ty, ny)) in enumerate((
            ((0, 1), (3, 3, 16), (18, 2, 1)),
            ((0, -1), (3, 3, 16), (5, 21, 1)),
            ((1, 0), (17, 1, 1), (4, 4, 16)),
            ((-1, 0), (4, 20, 1), (4, 4, 16)),
        ))
    ]
    for copy in h0:
        copy.start()

    landed_plane(C3, cas, car)
    start_z(C3, cbs, cbr)

    for copy in c1:
        copy.wait_recv()
    coefficients(C1, CX1, CY1, CZ1, W1, 24, 2)
    for k in range(3):
        C2[4 * k : 4 * k + 4, 0:12] = restrict_one(C1, 8 * k, 4, 0, 24, 0.125 * 0.25)
    coefficients(C2, CX2, CY2, CZ2, W2, 12, True)

    for copy in b1:
        copy.wait_recv()

    def from_zero(to_ref, b_ref, w_ref, lo, hi):
        to_ref[lo:hi] = w_ref[lo:hi] * b_ref[lo:hi]

    one = (B1, CX1, CY1, CZ1)
    from_zero(VA1, B1, W1, 2, 22)
    sweep(VA1, VB1, *one, W1, 3, 21, 2)
    flux_loop(VB1, *one, 4, 20, lambda x, v, r: put(R1, x, r), 2)
    B2[2:10, 0:12] = restrict_one(R1, 4, 8, 0, 24, 0.125)

    two = (B2, CX2, CY2, CZ2)
    from_zero(VA2, B2, W2, 2, 10)
    sweep(VA2, VB2, *two, W2, 3, 9, True)
    flux_loop(VB2, *two, 4, 8, lambda x, v, r: put(R2, x, r), True)
    B3[gy + 1, pl.ds(gx, 1), :] = restrict_two(R2, 0.125)
    start_plane(B3, bas, bar)
    B2H[4:8, 4:8] = B2[4:8, 4:8]
    V2H[4:8, 4:8] = VB2[4:8, 4:8]
    h2 = exchange(B2H, (4, 4), 4, 4, h2s.at[0], h2r.at[0]) + exchange(V2H, (4, 4), 4, 4, h2s.at[1], h2r.at[1])
    for copy in h2:
        copy.start()

    landed_z(C3, cbs, cbr)
    wrap_rows(C3)
    whole_coefficients(THREE, C3, K3)
    C4[1 : GY + 1] = coarsen_lanes(C3[1 : GY + 1]) * (0.125 * 0.25)
    wrap_rows(C4)
    whole_coefficients(FOUR, C4, K4)

    landed_plane(B3, bas, bar)
    start_z(B3, bbs, bbr)
    landed_z(B3, bbs, bbr)

    V3A[1 : GY + 1] = K3[7] * B3[1 : GY + 1]
    wrap_rows(V3A)
    whole_sweep(THREE, V3A, V3B, B3, K3)

    def residual(g, v, s):
        r = B3[pl.ds(g + 1, CH)] + s - K3[6, pl.ds(g, CH)] * v
        B4[pl.ds(g + 1, CH)] = coarsen_lanes(r) * 0.125

    whole_sum(THREE, V3B, K3, residual)

    b4 = B4[1 : GY + 1]
    b4 = b4 - jnp.sum(jnp.sum(b4, axis=0), keepdims=True) * (1.0 / (GY * GX * 128))
    B4[1 : GY + 1] = b4
    V4A[1 : GY + 1] = K4[7] * b4
    wrap_rows(V4A)
    here, there = V4A, V4B
    for _ in range(7):
        whole_sweep(FOUR, here, there, B4, K4)
        here, there = there, here

    V3B[...] = V3B[...] + here[...]
    whole_sweep(THREE, V3B, V3A, B3, K3)
    whole_sweep(THREE, V3A, V3B, B3, K3)

    near = [
        pltpu.roll(V3B[lax.rem(gy + j - 1 + GY, GY) + 1], lax.rem(1 - gx + GX, GX), 0) for j in range(3)
    ]
    u = mm(jnp.concatenate(near, axis=0), MP3[...])
    for copy in h2:
        copy.wait_recv()
    pair = lax.broadcasted_iota(jnp.int32, (16, 128), 0) // 2
    for x3 in range(6):
        i, dx = x3 // 2, x3 % 2
        rise = jnp.zeros((16, 128), F32)
        for y3 in range(6):
            j, g = y3 // 2, 2 * dx + y3 % 2
            rise = jnp.where(pair == y3, u[8 * j + i : 8 * j + i + 1, 128 * g : 128 * g + 128], rise)
        for x in (2 * x3, 2 * x3 + 1):
            VA2[x] = V2H[x] + rise
    two = (B2H, CX2, CY2, CZ2)
    sweep(VA2, R2, *two, W2, 1, 11, True)
    sweep(R2, VA2, *two, W2, 2, 10, True)

    for k in range(8):
        rows = VA2[2 + k, 0:12, :]
        TP1[k, pl.ds(0, 12, stride=2), :] = rows
        TP1[k, pl.ds(1, 12, stride=2), :] = rows
    TR[0:8] = mm(TP1[...].reshape(8 * 24, 128), MP2[...]).reshape(8, 24, 128)
    for x in range(5, 19):
        VA1[x] = VB1[x] + TR[x // 2 - 2]
    sweep(VA1, R1, *one, W1, 6, 18, 2)
    sweep(R1, VA1, *one, W1, 7, 17, 2)

    for k in range(10):
        rows = VA1[7 + k, 7:17, :]
        TP0[k, pl.ds(2, 10, stride=2), :] = rows
        TP0[k, pl.ds(3, 10, stride=2), :] = rows
    u = mm(TP0[...].reshape(10 * 24, 128), MP1[...])
    for h in range(2):
        PE0[:, h] = u[:, 128 * h : 128 * h + 128].reshape(10, 24, 128)
    for copy in h0:
        copy.wait_recv()
    row = lax.broadcasted_iota(jnp.int32, (24, 128), 0)
    outer = (row == 2) | (row == 21)

    def raise_slab(x, carry):
        for h in range(2):
            VA0[x, h] = jnp.where(outer, VH[x, h], VB0[x, h]) + PE0[lax.div(x - 1, 2), h]
        return carry

    lax.fori_loop(2, 20, raise_slab, 0, unroll=2)
    for x in (1, 20):
        for h in range(2):
            VA0[x, h] = VH[x, h] + PE0[(x - 1) // 2, h]
    for copy in e0c + e0v + e0b:
        copy.wait_send()
    sweep(VA0, V0, *zero, W0, 2, 20, 2)

    def last(x, v, r):
        s = add(v, mul(get(W0, x), r))
        for h in range(2):
            out_ref[x - 3, :, 128 * h : 128 * h + 128] = s[h][4:20]

    flux_loop(V0, *zero, 3, 19, last, 2)

    for copy in c1 + b1 + h0 + h2:
        copy.wait_send()
    sent(C3, cas, car, cbs, cbr)
    sent(B3, bas, bar, bbs, bbr)


def solution(mesh):
    def vmem(*shape):
        return pltpu.VMEM(shape, F32)

    def half(*shape):
        return pltpu.VMEM(shape, BF16)

    dma = pltpu.SemaphoreType.DMA
    scratch = (
        [vmem(22, 2, 24, 128)] * 10
        + [vmem(8, 24, 128), vmem(10, 2, 24, 128), vmem(10, 24, 128)]
        + [vmem(24, 24, 128)] * 9
        + [vmem(8, 24, 128)]
        + [vmem(12, 16, 128)] * 11
        + [vmem(GY + 2, GX, 128)] * 4
        + [vmem(8, GY, GX, 128)]
        + [vmem(GY + 2, GX, 128)] * 4
        + [vmem(8, GY, GX, 128)]
        + [half(384, 128), half(128, 128), half(128, 256), half(128, 128), half(128, 512)]
        + [dma((6,)), dma((3, 8)), dma((3, 8))]
        + [dma((8,))] * 4
        + [dma((4,))] * 2
        + [dma((2, 8))] * 2
        + [dma((GX * NYC,)), dma((GX * NYC,)), dma((NZC,)), dma((NZC,))] * 2
    )

    def step(source, conductivity, guess):
        return pl.pallas_call(
            kernel,
            out_shape=jax.ShapeDtypeStruct(source.shape, F32),
            in_specs=[pl.BlockSpec(memory_space=pl.ANY)] * 3,
            out_specs=pl.BlockSpec(memory_space=pltpu.VMEM),
            scratch_shapes=scratch,
            compiler_params=pltpu.CompilerParams(
                collective_id=0, has_side_effects=True, vmem_limit_bytes=40 * 2**20
            ),
            name="vcycle",
        )(source, conductivity, guess)

    spec = P("gx", "gy", None)
    return jax.shard_map(step, mesh=mesh, in_specs=(spec, spec, spec), out_specs=spec, check_vma=False)
```

```python
import jax
import jax.numpy as jnp
from jax import lax
from jax.experimental import pallas as pl
from jax.experimental.pallas import tpu as pltpu
from jax.sharding import PartitionSpec as P

MESH = pl.DeviceIdType.MESH
F32, BF16 = jnp.float32, jnp.bfloat16
OMEGA = 0.8
GX, GY, NYC, NZC = 8, 32, 4, 8
EIGHT = [(0, 1), (0, -1), (1, 1), (1, -1), (-1, 1), (-1, -1), (1, 0), (-1, 0)]


def harmonic(a, b):
    return 2.0 * a * b / (a + b)


def mm(a, m):
    hi = a.astype(BF16)
    lo = (a - hi.astype(F32)).astype(BF16)
    return jnp.dot(hi, m, preferred_element_type=F32) + jnp.dot(lo, m, preferred_element_type=F32)


def zp(s):
    if len(s) == 1:
        return (pltpu.roll(s[0], 127, 1),)
    last = lax.broadcasted_iota(jnp.int32, s[0].shape, 1) == 127
    a, b = pltpu.roll(s[0], 127, 1), pltpu.roll(s[1], 127, 1)
    return (jnp.where(last, b, a), jnp.where(last, a, b))


def zm(s):
    if len(s) == 1:
        return (pltpu.roll(s[0], 1, 1),)
    first = lax.broadcasted_iota(jnp.int32, s[0].shape, 1) == 0
    a, b = pltpu.roll(s[0], 1, 1), pltpu.roll(s[1], 1, 1)
    return (jnp.where(first, b, a), jnp.where(first, a, b))


def yp(s):
    return tuple(pltpu.roll(a, a.shape[0] - 1, 0) for a in s)


def ym(s):
    return tuple(pltpu.roll(a, 1, 0) for a in s)


def each(f, *slabs):
    return tuple(f(*a) for a in zip(*slabs))


def get(ref, x):
    if len(ref.shape) == 4:
        return (ref[x, 0], ref[x, 1])
    return (ref[x],)


def put(ref, x, s):
    if len(ref.shape) == 4:
        ref[x, 0] = s[0]
        ref[x, 1] = s[1]
    else:
        ref[x] = s[0]


def add(a, b):
    return each(lambda p, q: p + q, a, b)


def sub(a, b):
    return each(lambda p, q: p - q, a, b)


def mul(a, b):
    return each(lambda p, q: p * q, a, b)


def coefficients(c_ref, cx_ref, cy_ref, cz_ref, w_ref, slabs, unroll):
    c = get(c_ref, 0)
    n = get(c_ref, 1)
    first = each(harmonic, c, n)
    put(cx_ref, 0, first)

    def body(x, carry):
        c, before = carry
        n = get(c_ref, x + 1)
        ex = each(harmonic, c, n)
        ey = each(harmonic, c, yp(c))
        ez = each(harmonic, c, zp(c))
        d = add(add(add(ex, before), add(ey, ym(ey))), add(ez, zm(ez)))
        put(cx_ref, x, ex)
        put(cy_ref, x, ey)
        put(cz_ref, x, ez)
        put(w_ref, x, each(lambda p: OMEGA / p, d))
        return n, ex

    lax.fori_loop(1, slabs - 1, body, (n, first), unroll=unroll)


def flux_loop(v_ref, b_ref, cx_ref, cy_ref, cz_ref, lo, hi, emit, unroll):
    v = get(v_ref, lo)
    before = mul(get(cx_ref, lo - 1), sub(v, get(v_ref, lo - 1)))

    def body(x, carry):
        v, before = carry
        n = get(v_ref, x + 1)
        tx = mul(get(cx_ref, x), sub(n, v))
        ty = mul(get(cy_ref, x), sub(yp(v), v))
        tz = mul(get(cz_ref, x), sub(zp(v), v))
        r = add(add(sub(tx, before), sub(ty, ym(ty))), sub(tz, zm(tz)))
        emit(x, v, add(get(b_ref, x), r))
        return n, tx

    lax.fori_loop(lo, hi, body, (v, before), unroll=unroll)


def sweep(v_ref, to_ref, b_ref, cx_ref, cy_ref, cz_ref, w_ref, lo, hi, unroll):
    def emit(x, v, r):
        put(to_ref, x, add(v, mul(get(w_ref, x), r)))

    flux_loop(v_ref, b_ref, cx_ref, cy_ref, cz_ref, lo, hi, emit, unroll)


def lane(shape):
    return lax.broadcasted_iota(jnp.int32, shape, len(shape) - 1)


def three_zp(v):
    return jnp.where(lane(v.shape) % 32 == 31, pltpu.roll(v, 31, 2), pltpu.roll(v, 127, 2))


def three_zm(v):
    return jnp.where(lane(v.shape) % 32 == 0, pltpu.roll(v, 97, 2), pltpu.roll(v, 1, 2))


def three_xp(v):
    r = pltpu.roll(v, 64, 2)
    return jnp.where(lane(v.shape) < 64, r, pltpu.roll(r, GX - 1, 1))


def three_xm(v):
    r = pltpu.roll(v, 64, 2)
    return jnp.where(lane(v.shape) < 64, pltpu.roll(r, 1, 1), r)


def three_y(v):
    up, down = pltpu.roll(v, 96, 2), pltpu.roll(v, 32, 2)
    first = lane(v[1:-1].shape) % 64 < 32
    return (jnp.where(first, up[1:-1], down[2:]), jnp.where(first, up[:-2], down[1:-1]))


def four_zp(v):
    return pltpu.roll(v, 126, 2)


def four_zm(v):
    return pltpu.roll(v, 2, 2)


def four_xp(v):
    return pltpu.roll(v, GX - 1, 1)


def four_xm(v):
    return pltpu.roll(v, 1, 1)


def four_y(v):
    return v[2:], v[:-2]


THREE = (three_xp, three_xm, three_y, three_zp, three_zm)
FOUR = (four_xp, four_xm, four_y, four_zp, four_zm)
CH = 16
UN = 8


def wrap_rows(ref):
    ref[0] = ref[GY]
    ref[GY + 1] = ref[1]


def whole_coefficients(level, c_ref, k_ref):
    xp, xm, y, zplus, zminus = level

    def body(i, carry):
        g = i * CH
        ext = c_ref[pl.ds(g, CH + 2)]
        c = ext[1:-1]
        up, down = y(ext)
        ex = harmonic(c, xp(c))
        ez = harmonic(c, zplus(c))
        ey, wy = harmonic(c, up), harmonic(down, c)
        wx, wz = xm(ex), zminus(ez)
        d = (ex + wx) + (ey + wy) + (ez + wz)
        for j, value in enumerate((ex, wx, ey, wy, ez, wz, d, OMEGA / d)):
            k_ref[j, pl.ds(g, CH)] = value
        return carry

    lax.fori_loop(0, GY // CH, body, 0, unroll=True)


def whole_sum(level, v_ref, k_ref, emit):
    xp, xm, y, zplus, zminus = level

    def body(i, carry):
        g = i * CH
        ext = v_ref[pl.ds(g, CH + 2)]
        v = ext[1:-1]
        up, down = y(ext)
        k = [k_ref[j, pl.ds(g, CH)] for j in range(6)]
        s = (k[0] * xp(v) + k[1] * xm(v)) + (k[2] * up + k[3] * down)
        emit(g, v, s + (k[4] * zplus(v) + k[5] * zminus(v)))
        return carry

    lax.fori_loop(0, GY // CH, body, 0, unroll=True)


def whole_sweep(level, v_ref, to_ref, b_ref, k_ref):
    def emit(g, v, s):
        to_ref[pl.ds(g + 1, CH)] = (1.0 - OMEGA) * v + k_ref[7, pl.ds(g, CH)] * (b_ref[pl.ds(g + 1, CH)] + s)

    whole_sum(level, v_ref, k_ref, emit)
    wrap_rows(to_ref)


def coarsen_lanes(v):
    s = v + pltpu.roll(v, 64, 2)
    s = s + pltpu.roll(s, 32, 2)
    return s + jnp.where(lane(v.shape) % 2 == 0, pltpu.roll(s, 127, 2), pltpu.roll(s, 1, 2))


def kernel(
    src_ref, cond_ref, guess_ref, out_ref,
    V0, B0, C0, CX0, CY0, CZ0, W0, VA0, VB0, VH, TR, PE0, TP0,
    C1, CX1, CY1, CZ1, W1, B1, VA1, VB1, R1, TP1,
    C2, CX2, CY2, CZ2, W2, B2, VA2, VB2, R2, B2H, V2H,
    C3, B3, V3A, V3B, K3, C4, B4, V4A, V4B, K4,
    MR, M3, MP1, MP2, MP3, ROWS,
    lsem, e0s, e0r, c1s, c1r, b1s, b1r, h0s, h0r, h2s, h2r, cg, bg,
):
    gx, gy = lax.axis_index("gx"), lax.axis_index("gy")
    yc, zc = lax.rem(gy, NYC), lax.div(gy, NYC)

    def beside(dx, dy):
        return (lax.rem(gx + dx + GX, GX), lax.rem(gy + dy + GY, GY))

    def in_plane(k):
        return (lax.rem(gx + lax.div(k, NYC), GX), zc * NYC + lax.rem(yc + lax.rem(k, NYC), NYC))

    def along_z(k):
        return (gx, lax.rem(zc + k, NZC) * NYC + yc)

    def remote(src, dst, send, recv, device):
        return pltpu.make_async_remote_copy(
            src_ref=src, dst_ref=dst, send_sem=send, recv_sem=recv, device_id=device, device_id_type=MESH
        )

    loads = []
    for i, (ref, to) in enumerate(((cond_ref, C0), (guess_ref, V0), (src_ref, B0))):
        for h in range(2):
            loads.append(
                pltpu.make_async_copy(
                    ref.at[:, :, pl.ds(128 * h, 128)],
                    to.at[pl.ds(3, 16), h, pl.ds(4, 16), :],
                    lsem.at[2 * i + h],
                )
            )
    for copy in loads:
        copy.start()

    barrier = pltpu.get_barrier_semaphore()
    for dx, dy in EIGHT:
        pl.semaphore_signal(barrier, inc=1, device_id=beside(dx, dy), device_id_type=MESH)

    def greet_plane(k, carry):
        pl.semaphore_signal(barrier, inc=1, device_id=in_plane(k), device_id_type=MESH)
        return carry

    def greet_z(k, carry):
        pl.semaphore_signal(barrier, inc=1, device_id=along_z(k), device_id_type=MESH)
        return carry

    lax.fori_loop(1, GX * NYC, greet_plane, 0)
    lax.fori_loop(1, NZC, greet_z, 0)

    for copy in loads:
        copy.wait()
    pl.semaphore_wait(barrier, len(EIGHT) + GX * NYC - 1 + NZC - 1)

    def edge(base, extent, step, width):
        if step == 0:
            return base, base, extent
        if step == 1:
            return base + extent - width, base - width, width
        return base, base + extent, width

    def block_copy(ref, base, extent, step, width, send, recv):
        sx, tx, nx = edge(base[0], extent, step[0], width)
        sy, ty, ny = edge(base[1], extent, step[1], width)
        if len(ref.shape) == 4:
            src, dst = ref.at[pl.ds(sx, nx), :, pl.ds(sy, ny), :], ref.at[pl.ds(tx, nx), :, pl.ds(ty, ny), :]
        else:
            src, dst = ref.at[pl.ds(sx, nx), pl.ds(sy, ny), :], ref.at[pl.ds(tx, nx), pl.ds(ty, ny), :]
        return remote(src, dst, send, recv, beside(*step))

    def exchange(ref, base, extent, width, send, recv, corner=None):
        return [
            block_copy(ref, base, extent, o, corner if corner and o[0] and o[1] else width, send.at[i], recv.at[i])
            for i, o in enumerate(EIGHT)
        ]

    e0c = exchange(C0, (3, 4), 16, 3, e0s.at[0], e0r.at[0])
    e0v = exchange(V0, (3, 4), 16, 3, e0s.at[1], e0r.at[1])
    e0b = exchange(B0, (3, 4), 16, 2, e0s.at[2], e0r.at[2])
    for faces in ((0, 1), (2, 3, 4, 5), (6, 7)):
        for copies in (e0c, e0v, e0b):
            for i in faces:
                copies[i].start()

    def matrix(rows, columns, rule):
        r = lax.broadcasted_iota(jnp.int32, (rows, columns), 0)
        c = lax.broadcasted_iota(jnp.int32, (rows, columns), 1)
        return jnp.where(rule(r, c), 1.0, 0.0).astype(BF16)

    MR[0:256] = matrix(256, 128, lambda r, c: r // 2 == c)
    MR[256:384] = matrix(128, 128, lambda r, c: r // 2 == c % 64)
    M3[...] = matrix(128, 128, lambda r, c: (r < 64) & (r // 2 == c % 32))
    MP1[...] = matrix(128, 256, lambda r, c: r == c // 2)
    MP2[...] = matrix(128, 128, lambda r, c: r == c // 2)
    MP3[...] = matrix(128, 512, lambda r, c: (r // 32 == c // 128) & (r % 32 == (c % 64) // 2))

    def restrict_zero(ref, scale):
        pairs = [
            jnp.concatenate([ref[3 + 2 * k, h, 4:20] + ref[4 + 2 * k, h, 4:20] for h in range(2)], axis=1)
            for k in range(8)
        ]
        TR[0:8, 0:16] = mm(jnp.concatenate(pairs, axis=0), MR[0:256]).reshape(8, 16, 128)
        return (TR[0:8, pl.ds(0, 8, stride=2), :] + TR[0:8, pl.ds(1, 8, stride=2), :]) * scale

    def restrict_one(ref, x0, count, y0, rows, scale):
        pairs = [ref[x0 + 2 * k, y0 : y0 + rows] + ref[x0 + 1 + 2 * k, y0 : y0 + rows] for k in range(count)]
        TR[0:count, 0:rows] = mm(jnp.concatenate(pairs, axis=0), MR[256:384]).reshape(count, rows, 128)
        half = rows // 2
        return (TR[0:count, pl.ds(0, half, stride=2), :] + TR[0:count, pl.ds(1, half, stride=2), :]) * scale

    def restrict_two(ref, scale):
        pairs = jnp.concatenate([ref[4] + ref[5], ref[6] + ref[7]], axis=0)
        s = mm(pairs, M3[...]) * scale
        group = lax.broadcasted_iota(jnp.int32, (1, 128), 1) // 32
        row = jnp.zeros((1, 128), F32)
        for g in range(4):
            at = 16 * (g // 2) + 4 + 2 * (g % 2)
            row = jnp.where(group == g, s[at : at + 1] + s[at + 1 : at + 2], row)
        return row

    def plane_copy(ref, k, sems):
        part = ref.at[gy + 1, pl.ds(gx, 1), :]
        return remote(part, part, sems.at[0], sems.at[1], in_plane(k))

    def z_copy(ref, k, sems):
        part = ref.at[pl.ds(zc * NYC + 1, NYC)]
        return remote(part, part, sems.at[2], sems.at[3], along_z(k))

    def start_plane(ref, sems):
        def go(k, carry):
            plane_copy(ref, k, sems).start()
            return carry

        lax.fori_loop(1, GX * NYC, go, 0, unroll=True)

    def start_z(ref, sems):
        for k in range(1, NZC):
            z_copy(ref, k, sems).start()

    def all_bytes(ref, kind, sem):
        part = ROWS if kind == 0 else ref.at[pl.ds(1, GY - NYC)]
        pltpu.make_async_copy(part, part, sem).wait()

    def landed_plane(ref, sems):
        all_bytes(ref, 0, sems.at[1])

    def landed_z(ref, sems):
        all_bytes(ref, 1, sems.at[3])

    def sent(ref, sems):
        all_bytes(ref, 0, sems.at[0])
        all_bytes(ref, 1, sems.at[2])

    C1[8:16, 8:16] = restrict_zero(C0, 0.125 * 0.25)
    c1 = exchange(C1, (8, 8), 8, 8, c1s, c1r)
    for copy in c1:
        copy.start()
    C2[4:8, 4:8] = restrict_one(C1, 8, 4, 8, 8, 0.125 * 0.25)
    C3[gy + 1, pl.ds(gx, 1), :] = restrict_two(C2, 0.125 * 0.25)
    start_plane(C3, cg)

    for copy in e0c:
        copy.wait_recv()
    coefficients(C0, CX0, CY0, CZ0, W0, 22, UN)
    for copy in e0v + e0b:
        copy.wait_recv()
    zero = (B0, CX0, CY0, CZ0)
    sweep(V0, VA0, *zero, W0, 1, 21, UN)
    sweep(VA0, VB0, *zero, W0, 2, 20, UN)
    flux_loop(VB0, *zero, 3, 19, lambda x, v, r: put(VA0, x, r), UN)
    B1[8:16, 8:16] = restrict_zero(VA0, 0.125)
    b1 = exchange(B1, (8, 8), 8, 6, b1s, b1r, 5)
    for copy in b1:
        copy.start()

    h0 = [
        remote(VB0.at[pl.ds(sx, nx), :, pl.ds(sy, ny), :], VH.at[pl.ds(tx, nx), :, pl.ds(ty, ny), :],
               h0s.at[i], h0r.at[i], beside(*o))
        for i, (o, (sx, tx, nx), (sy, ty, ny)) in enumerate((
            ((0, 1), (3, 3, 16), (18, 2, 1)),
            ((0, -1), (3, 3, 16), (5, 21, 1)),
            ((1, 0), (17, 1, 1), (4, 4, 16)),
            ((-1, 0), (4, 20, 1), (4, 4, 16)),
        ))
    ]
    for copy in h0:
        copy.start()

    landed_plane(C3, cg)
    start_z(C3, cg)

    for copy in c1:
        copy.wait_recv()
    coefficients(C1, CX1, CY1, CZ1, W1, 24, UN)
    for k in range(3):
        C2[4 * k : 4 * k + 4, 0:12] = restrict_one(C1, 8 * k, 4, 0, 24, 0.125 * 0.25)
    coefficients(C2, CX2, CY2, CZ2, W2, 12, True)

    for copy in b1:
        copy.wait_recv()

    def from_zero(to_ref, b_ref, w_ref, lo, hi):
        to_ref[lo:hi] = w_ref[lo:hi] * b_ref[lo:hi]

    one = (B1, CX1, CY1, CZ1)
    from_zero(VA1, B1, W1, 2, 22)
    sweep(VA1, VB1, *one, W1, 3, 21, UN)
    flux_loop(VB1, *one, 4, 20, lambda x, v, r: put(R1, x, r), UN)
    B2[2:10, 0:12] = restrict_one(R1, 4, 8, 0, 24, 0.125)

    two = (B2, CX2, CY2, CZ2)
    from_zero(VA2, B2, W2, 2, 10)
    sweep(VA2, VB2, *two, W2, 3, 9, True)
    flux_loop(VB2, *two, 4, 8, lambda x, v, r: put(R2, x, r), True)
    B3[gy + 1, pl.ds(gx, 1), :] = restrict_two(R2, 0.125)
    start_plane(B3, bg)
    B2H[4:8, 4:8] = B2[4:8, 4:8]
    V2H[4:8, 4:8] = VB2[4:8, 4:8]
    h2 = exchange(B2H, (4, 4), 4, 4, h2s.at[0], h2r.at[0]) + exchange(V2H, (4, 4), 4, 4, h2s.at[1], h2r.at[1])
    for copy in h2:
        copy.start()

    landed_z(C3, cg)
    wrap_rows(C3)
    whole_coefficients(THREE, C3, K3)
    C4[1 : GY + 1] = coarsen_lanes(C3[1 : GY + 1]) * (0.125 * 0.25)
    wrap_rows(C4)
    whole_coefficients(FOUR, C4, K4)

    landed_plane(B3, bg)
    start_z(B3, bg)
    landed_z(B3, bg)

    V3A[1 : GY + 1] = K3[7] * B3[1 : GY + 1]
    wrap_rows(V3A)
    whole_sweep(THREE, V3A, V3B, B3, K3)

    def residual(g, v, s):
        r = B3[pl.ds(g + 1, CH)] + s - K3[6, pl.ds(g, CH)] * v
        B4[pl.ds(g + 1, CH)] = coarsen_lanes(r) * 0.125

    whole_sum(THREE, V3B, K3, residual)

    b4 = B4[1 : GY + 1]
    b4 = b4 - jnp.sum(jnp.sum(b4, axis=0), keepdims=True) * (1.0 / (GY * GX * 128))
    B4[1 : GY + 1] = b4
    V4A[1 : GY + 1] = K4[7] * b4
    wrap_rows(V4A)
    here, there = V4A, V4B
    for _ in range(7):
        whole_sweep(FOUR, here, there, B4, K4)
        here, there = there, here

    V3B[...] = V3B[...] + here[...]
    whole_sweep(THREE, V3B, V3A, B3, K3)
    whole_sweep(THREE, V3A, V3B, B3, K3)

    near = [
        pltpu.roll(V3B[lax.rem(gy + j - 1 + GY, GY) + 1], lax.rem(1 - gx + GX, GX), 0) for j in range(3)
    ]
    u = mm(jnp.concatenate(near, axis=0), MP3[...])
    for copy in h2:
        copy.wait_recv()
    pair = lax.broadcasted_iota(jnp.int32, (16, 128), 0) // 2
    for x3 in range(6):
        i, dx = x3 // 2, x3 % 2
        rise = jnp.zeros((16, 128), F32)
        for y3 in range(6):
            j, g = y3 // 2, 2 * dx + y3 % 2
            rise = jnp.where(pair == y3, u[8 * j + i : 8 * j + i + 1, 128 * g : 128 * g + 128], rise)
        for x in (2 * x3, 2 * x3 + 1):
            VA2[x] = V2H[x] + rise
    two = (B2H, CX2, CY2, CZ2)
    sweep(VA2, R2, *two, W2, 1, 11, True)
    sweep(R2, VA2, *two, W2, 2, 10, True)

    for k in range(8):
        rows = VA2[2 + k, 0:12, :]
        TP1[k, pl.ds(0, 12, stride=2), :] = rows
        TP1[k, pl.ds(1, 12, stride=2), :] = rows
    TR[0:8] = mm(TP1[...].reshape(8 * 24, 128), MP2[...]).reshape(8, 24, 128)
    for x in range(5, 19):
        VA1[x] = VB1[x] + TR[x // 2 - 2]
    sweep(VA1, R1, *one, W1, 6, 18, UN)
    sweep(R1, VA1, *one, W1, 7, 17, UN)

    for k in range(10):
        rows = VA1[7 + k, 7:17, :]
        TP0[k, pl.ds(2, 10, stride=2), :] = rows
        TP0[k, pl.ds(3, 10, stride=2), :] = rows
    u = mm(TP0[...].reshape(10 * 24, 128), MP1[...])
    for h in range(2):
        PE0[:, h] = u[:, 128 * h : 128 * h + 128].reshape(10, 24, 128)
    for copy in h0:
        copy.wait_recv()
    row = lax.broadcasted_iota(jnp.int32, (24, 128), 0)
    outer = (row == 2) | (row == 21)

    def raise_slab(x, carry):
        for h in range(2):
            VA0[x, h] = jnp.where(outer, VH[x, h], VB0[x, h]) + PE0[lax.div(x - 1, 2), h]
        return carry

    lax.fori_loop(2, 20, raise_slab, 0, unroll=UN)
    for x in (1, 20):
        for h in range(2):
            VA0[x, h] = VH[x, h] + PE0[(x - 1) // 2, h]
    for copy in e0c + e0v + e0b:
        copy.wait_send()
    sweep(VA0, V0, *zero, W0, 2, 20, UN)

    def last(x, v, r):
        s = add(v, mul(get(W0, x), r))
        for h in range(2):
            out_ref[x - 3, :, 128 * h : 128 * h + 128] = s[h][4:20]

    flux_loop(V0, *zero, 3, 19, last, UN)

    for copy in c1 + b1 + h0 + h2:
        copy.wait_send()
    sent(C3, cg)
    sent(B3, bg)


def solution(mesh):
    def vmem(*shape):
        return pltpu.VMEM(shape, F32)

    def half(*shape):
        return pltpu.VMEM(shape, BF16)

    dma = pltpu.SemaphoreType.DMA
    scratch = (
        [vmem(22, 2, 24, 128)] * 10
        + [vmem(8, 24, 128), vmem(10, 2, 24, 128), vmem(10, 24, 128)]
        + [vmem(24, 24, 128)] * 9
        + [vmem(8, 24, 128)]
        + [vmem(12, 16, 128)] * 11
        + [vmem(GY + 2, GX, 128)] * 4
        + [vmem(8, GY, GX, 128)]
        + [vmem(GY + 2, GX, 128)] * 4
        + [vmem(8, GY, GX, 128)]
        + [half(384, 128), half(128, 128), half(128, 256), half(128, 128), half(128, 512)]
        + [vmem(GX * NYC - 1, 128)]
        + [dma((6,)), dma((3, 8)), dma((3, 8))]
        + [dma((8,))] * 4
        + [dma((4,))] * 2
        + [dma((2, 8))] * 2
        + [dma((4,))] * 2
    )

    def step(source, conductivity, guess):
        return pl.pallas_call(
            kernel,
            out_shape=jax.ShapeDtypeStruct(source.shape, F32),
            in_specs=[pl.BlockSpec(memory_space=pl.ANY)] * 3,
            out_specs=pl.BlockSpec(memory_space=pltpu.VMEM),
            scratch_shapes=scratch,
            compiler_params=pltpu.CompilerParams(
                collective_id=0, has_side_effects=True, vmem_limit_bytes=54848 * 2**10
            ),
            name="vcycle",
        )(source, conductivity, guess)

    spec = P("gx", "gy", None)
    return jax.shard_map(step, mesh=mesh, in_specs=(spec, spec, spec), out_specs=spec, check_vma=False)
```

```python
import jax
import jax.numpy as jnp
from jax import lax
from jax.experimental import pallas as pl
from jax.experimental.pallas import tpu as pltpu
from jax.sharding import PartitionSpec as P

MESH = pl.DeviceIdType.MESH
F32, BF16 = jnp.float32, jnp.bfloat16
OMEGA = 0.8
GX, GY, NYC, NZC = 8, 32, 4, 8
FAR_FIRST = sorted(
    ((dx, dy) for dx in range(GX) for dy in range(NYC) if dx or dy),
    key=lambda o: -(min(o[0], GX - o[0]) + 2 * min(o[1], NYC - o[1])),
)
EIGHT = [(0, 1), (0, -1), (1, 1), (1, -1), (-1, 1), (-1, -1), (1, 0), (-1, 0)]


def harmonic(a, b):
    return 2.0 * a * b / (a + b)


def mm(a, m):
    hi = a.astype(BF16)
    lo = (a - hi.astype(F32)).astype(BF16)
    return jnp.dot(hi, m, preferred_element_type=F32) + jnp.dot(lo, m, preferred_element_type=F32)


def zp(s):
    if len(s) == 1:
        return (pltpu.roll(s[0], 127, 1),)
    last = lax.broadcasted_iota(jnp.int32, s[0].shape, 1) == 127
    a, b = pltpu.roll(s[0], 127, 1), pltpu.roll(s[1], 127, 1)
    return (jnp.where(last, b, a), jnp.where(last, a, b))


def zm(s):
    if len(s) == 1:
        return (pltpu.roll(s[0], 1, 1),)
    first = lax.broadcasted_iota(jnp.int32, s[0].shape, 1) == 0
    a, b = pltpu.roll(s[0], 1, 1), pltpu.roll(s[1], 1, 1)
    return (jnp.where(first, b, a), jnp.where(first, a, b))


def yp(s):
    return tuple(pltpu.roll(a, a.shape[0] - 1, 0) for a in s)


def ym(s):
    return tuple(pltpu.roll(a, 1, 0) for a in s)


def each(f, *slabs):
    return tuple(f(*a) for a in zip(*slabs))


def get(ref, x):
    if len(ref.shape) == 4:
        return (ref[x, 0], ref[x, 1])
    return (ref[x],)


def put(ref, x, s):
    if len(ref.shape) == 4:
        ref[x, 0] = s[0]
        ref[x, 1] = s[1]
    else:
        ref[x] = s[0]


def add(a, b):
    return each(lambda p, q: p + q, a, b)


def sub(a, b):
    return each(lambda p, q: p - q, a, b)


def mul(a, b):
    return each(lambda p, q: p * q, a, b)


def steps_of(count, most):
    return max(n for n in range(1, most + 1) if count % n == 0)


def coefficients(c_ref, cx_ref, cy_ref, cz_ref, w_ref, slabs):
    c = get(c_ref, 0)
    n = get(c_ref, 1)
    first = each(harmonic, c, n)
    put(cx_ref, 0, first)

    def body(x, carry):
        c, before = carry
        n = get(c_ref, x + 1)
        ex = each(harmonic, c, n)
        ey = each(harmonic, c, yp(c))
        ez = each(harmonic, c, zp(c))
        d = add(add(add(ex, before), add(ey, ym(ey))), add(ez, zm(ez)))
        put(cx_ref, x, ex)
        put(cy_ref, x, ey)
        put(cz_ref, x, ez)
        put(w_ref, x, each(lambda p: OMEGA / p, d))
        return n, ex

    lax.fori_loop(1, slabs - 1, body, (n, first), unroll=steps_of(slabs - 2, UNROLL_FACES[len(c_ref.shape)]))


def flux_loop(v_ref, b_ref, cx_ref, cy_ref, cz_ref, lo, hi, emit):
    v = get(v_ref, lo)
    before = mul(get(cx_ref, lo - 1), sub(v, get(v_ref, lo - 1)))

    def body(x, carry):
        v, before = carry
        n = get(v_ref, x + 1)
        tx = mul(get(cx_ref, x), sub(n, v))
        ty = mul(get(cy_ref, x), sub(yp(v), v))
        tz = mul(get(cz_ref, x), sub(zp(v), v))
        r = add(add(sub(tx, before), sub(ty, ym(ty))), sub(tz, zm(tz)))
        emit(x, v, add(get(b_ref, x), r))
        return n, tx

    lax.fori_loop(lo, hi, body, (v, before), unroll=steps_of(hi - lo, UNROLL[len(v_ref.shape)]))


def sweep(v_ref, to_ref, b_ref, cx_ref, cy_ref, cz_ref, w_ref, lo, hi):
    def emit(x, v, r):
        put(to_ref, x, add(v, mul(get(w_ref, x), r)))

    flux_loop(v_ref, b_ref, cx_ref, cy_ref, cz_ref, lo, hi, emit)


def lane(shape):
    return lax.broadcasted_iota(jnp.int32, shape, len(shape) - 1)


def three_zp(v):
    return jnp.where(lane(v.shape) % 32 == 31, pltpu.roll(v, 31, 2), pltpu.roll(v, 127, 2))


def three_zm(v):
    return jnp.where(lane(v.shape) % 32 == 0, pltpu.roll(v, 97, 2), pltpu.roll(v, 1, 2))


def three_xp(v):
    r = pltpu.roll(v, 64, 2)
    return jnp.where(lane(v.shape) < 64, r, pltpu.roll(r, GX - 1, 1))


def three_xm(v):
    r = pltpu.roll(v, 64, 2)
    return jnp.where(lane(v.shape) < 64, pltpu.roll(r, 1, 1), r)


def three_y(v):
    up, down = pltpu.roll(v, 96, 2), pltpu.roll(v, 32, 2)
    first = lane(v[1:-1].shape) % 64 < 32
    return (jnp.where(first, up[1:-1], down[2:]), jnp.where(first, up[:-2], down[1:-1]))


def four_zp(v):
    return pltpu.roll(v, 126, 2)


def four_zm(v):
    return pltpu.roll(v, 2, 2)


def four_xp(v):
    return pltpu.roll(v, GX - 1, 1)


def four_xm(v):
    return pltpu.roll(v, 1, 1)


def four_y(v):
    return v[2:], v[:-2]


THREE = (three_xp, three_xm, three_y, three_zp, three_zm)
FOUR = (four_xp, four_xm, four_y, four_zp, four_zm)
UNROLL = {4: 10, 3: 20}
UNROLL_FACES = {4: 10, 3: 11}


def wrap_rows(ref):
    ref[0] = ref[GY]
    ref[GY + 1] = ref[1]


def chunks(lo, hi):
    parts = -(-(hi - lo) // 16)
    cuts = [lo + (hi - lo) * i // parts for i in range(parts + 1)]
    return list(zip(cuts[:-1], cuts[1:]))


def whole_coefficients(level, c_ref, k_ref):
    xp, xm, y, zplus, zminus = level
    for lo, hi in chunks(0, GY):
        ext = c_ref[lo : hi + 2]
        c = ext[1:-1]
        up, down = y(ext)
        ex = harmonic(c, xp(c))
        ez = harmonic(c, zplus(c))
        ey, wy = harmonic(c, up), harmonic(down, c)
        wx, wz = xm(ex), zminus(ez)
        d = (ex + wx) + (ey + wy) + (ez + wz)
        for j, value in enumerate((ex, wx, ey, wy, ez, wz, d, OMEGA / d)):
            k_ref[j, lo:hi] = value


def whole_sum(level, v_ref, k_ref, emit, first, last):
    xp, xm, y, zplus, zminus = level
    for lo, hi in chunks(first, last):
        ext = v_ref[lo : hi + 2]
        v = ext[1:-1]
        up, down = y(ext)
        k = [k_ref[j, lo:hi] for j in range(6)]
        s = (k[0] * xp(v) + k[1] * xm(v)) + (k[2] * up + k[3] * down)
        emit(lo, hi, v, s + (k[4] * zplus(v) + k[5] * zminus(v)))


def whole_sweep(level, v_ref, to_ref, b_ref, k_ref, first=0, last=GY):
    def emit(lo, hi, v, s):
        to_ref[lo + 1 : hi + 1] = (1.0 - OMEGA) * v + k_ref[7, lo:hi] * (b_ref[lo + 1 : hi + 1] + s)

    whole_sum(level, v_ref, k_ref, emit, first, last)
    if last - first == GY:
        wrap_rows(to_ref)


def coarsen_lanes(v):
    s = v + pltpu.roll(v, 64, 2)
    s = s + pltpu.roll(s, 32, 2)
    return s + jnp.where(lane(v.shape) % 2 == 0, pltpu.roll(s, 127, 2), pltpu.roll(s, 1, 2))


def kernel(
    src_ref, cond_ref, guess_ref, out_ref,
    V0, B0, C0, CX0, CY0, CZ0, W0, VA0, VB0, VH, TR, PE0, TP0,
    C1, CX1, CY1, CZ1, W1, B1, VA1, VB1, R1, TP1,
    C2, CX2, CY2, CZ2, W2, B2, VA2, VB2, R2, B2H, V2H,
    C3, B3, V3A, V3B, K3, C4, B4, V4A, V4B, K4, GC, GB,
    MR, M3, MP1, MP2, MP3, ROWS,
    lsem, e0s, e0r, c1s, c1r, b1s, b1r, h0s, h0r, h2s, h2r, cg, bg,
):
    gx, gy = lax.axis_index("gx"), lax.axis_index("gy")
    yc, zc = lax.rem(gy, NYC), lax.div(gy, NYC)

    def beside(dx, dy):
        return (lax.rem(gx + dx + GX, GX), lax.rem(gy + dy + GY, GY))

    def in_plane(k):
        return (lax.rem(gx + lax.div(k, NYC), GX), zc * NYC + lax.rem(yc + lax.rem(k, NYC), NYC))

    def along_z(k):
        return (gx, lax.rem(zc + k, NZC) * NYC + yc)

    def remote(src, dst, send, recv, device):
        return pltpu.make_async_remote_copy(
            src_ref=src, dst_ref=dst, send_sem=send, recv_sem=recv, device_id=device, device_id_type=MESH
        )

    loads = []
    for i, (ref, to) in enumerate(((cond_ref, C0), (guess_ref, V0), (src_ref, B0))):
        for h in range(2):
            loads.append(
                pltpu.make_async_copy(
                    ref.at[:, :, pl.ds(128 * h, 128)],
                    to.at[pl.ds(3, 16), h, pl.ds(4, 16), :],
                    lsem.at[2 * i + h],
                )
            )
    for copy in loads:
        copy.start()

    barrier = pltpu.get_barrier_semaphore()
    for dx, dy in EIGHT:
        pl.semaphore_signal(barrier, inc=1, device_id=beside(dx, dy), device_id_type=MESH)

    def greet_plane(k, carry):
        pl.semaphore_signal(barrier, inc=1, device_id=in_plane(k), device_id_type=MESH)
        return carry

    def greet_z(k, carry):
        pl.semaphore_signal(barrier, inc=1, device_id=along_z(k), device_id_type=MESH)
        return carry

    lax.fori_loop(1, GX * NYC, greet_plane, 0)
    lax.fori_loop(1, NZC, greet_z, 0)

    pl.semaphore_wait(barrier, len(EIGHT) + GX * NYC - 1 + NZC - 1)

    def edge(base, extent, step, width):
        if step == 0:
            return base, base, extent
        if step == 1:
            return base + extent - width, base - width, width
        return base, base + extent, width

    def block_copy(ref, base, extent, step, width, send, recv):
        sx, tx, nx = edge(base[0], extent, step[0], width)
        sy, ty, ny = edge(base[1], extent, step[1], width)
        if len(ref.shape) == 4:
            src, dst = ref.at[pl.ds(sx, nx), :, pl.ds(sy, ny), :], ref.at[pl.ds(tx, nx), :, pl.ds(ty, ny), :]
        else:
            src, dst = ref.at[pl.ds(sx, nx), pl.ds(sy, ny), :], ref.at[pl.ds(tx, nx), pl.ds(ty, ny), :]
        return remote(src, dst, send, recv, beside(*step))

    def exchange(ref, base, extent, width, send, recv, corner=None):
        return [
            block_copy(ref, base, extent, o, corner if corner and o[0] and o[1] else width, send.at[i], recv.at[i])
            for i, o in enumerate(EIGHT)
        ]

    e0c = exchange(C0, (3, 4), 16, 3, e0s.at[0], e0r.at[0], 2)
    e0v = exchange(V0, (3, 4), 16, 3, e0s.at[1], e0r.at[1], 2)
    e0b = exchange(B0, (3, 4), 16, 2, e0s.at[2], e0r.at[2], 1)
    for faces in ((0, 1), (2, 3, 4, 5), (6, 7)):
        for n, copies in enumerate((e0c, e0v, e0b)):
            if faces[0] == 0:
                loads[2 * n].wait()
                loads[2 * n + 1].wait()
            for i in faces:
                copies[i].start()

    def matrix(rows, columns, rule):
        r = lax.broadcasted_iota(jnp.int32, (rows, columns), 0)
        c = lax.broadcasted_iota(jnp.int32, (rows, columns), 1)
        return jnp.where(rule(r, c), 1.0, 0.0).astype(BF16)

    MR[0:256] = matrix(256, 128, lambda r, c: r // 2 == c)
    MR[256:384] = matrix(128, 128, lambda r, c: r // 2 == c % 64)
    M3[...] = matrix(128, 128, lambda r, c: (r < 64) & (r // 2 == c % 32))
    MP1[...] = matrix(128, 256, lambda r, c: r == c // 2)
    MP2[...] = matrix(128, 128, lambda r, c: r == c // 2)
    MP3[...] = matrix(128, 512, lambda r, c: (r // 32 == c // 128) & (r % 32 == (c % 64) // 2))

    def restrict_zero(ref, scale):
        pairs = [
            jnp.concatenate([ref[3 + 2 * k, h, 4:20] + ref[4 + 2 * k, h, 4:20] for h in range(2)], axis=1)
            for k in range(8)
        ]
        TR[0:8, 0:16] = mm(jnp.concatenate(pairs, axis=0), MR[0:256]).reshape(8, 16, 128)
        return (TR[0:8, pl.ds(0, 8, stride=2), :] + TR[0:8, pl.ds(1, 8, stride=2), :]) * scale

    def restrict_one(ref, x0, count, y0, rows, scale):
        pairs = [ref[x0 + 2 * k, y0 : y0 + rows] + ref[x0 + 1 + 2 * k, y0 : y0 + rows] for k in range(count)]
        TR[0:count, 0:rows] = mm(jnp.concatenate(pairs, axis=0), MR[256:384]).reshape(count, rows, 128)
        half = rows // 2
        return (TR[0:count, pl.ds(0, half, stride=2), :] + TR[0:count, pl.ds(1, half, stride=2), :]) * scale

    def restrict_two(ref, scale):
        pairs = jnp.concatenate([ref[4] + ref[5], ref[6] + ref[7]], axis=0)
        s = mm(pairs, M3[...]) * scale
        group = lax.broadcasted_iota(jnp.int32, (1, 128), 1) // 32
        row = jnp.zeros((1, 128), F32)
        for g in range(4):
            at = 16 * (g // 2) + 4 + 2 * (g % 2)
            row = jnp.where(group == g, s[at : at + 1] + s[at + 1 : at + 2], row)
        return row

    def z_copy(ref, k, sems):
        src = ref.at[NZC // 2, yc, pl.ds(gx, 1), :]
        dst = ref.at[(NZC // 2 - k) % NZC, yc, pl.ds(gx, 1), :]
        return remote(src, dst, sems.at[0], sems.at[1], along_z(k))

    def plane_copy(ref, dx, dy, sems):
        part = ref.at[:, yc, pl.ds(gx, 1), :]
        return remote(part, part, sems.at[2], sems.at[3], in_plane(dx * NYC + dy))

    def start_z(ref, sems):
        for k in (4, 3, 5, 2, 6, 1, 7):
            z_copy(ref, k, sems).start()

    def start_plane(ref, sems):
        for dx, dy in FAR_FIRST:
            plane_copy(ref, dx, dy, sems).start()

    def all_bytes(kind, sem):
        part = ROWS.at[0, pl.ds(0, NZC - 1), :] if kind == 0 else ROWS
        pltpu.make_async_copy(part, part, sem).wait()

    def landed_z(sems):
        all_bytes(0, sems.at[1])

    def landed_plane(sems):
        all_bytes(1, sems.at[3])

    def sent(sems):
        all_bytes(0, sems.at[0])
        all_bytes(1, sems.at[2])

    C1[8:16, 8:16] = restrict_zero(C0, 0.125 * 0.25)
    c1 = exchange(C1, (8, 8), 8, 8, c1s, c1r)
    for copy in c1:
        copy.start()
    C2[4:8, 4:8] = restrict_one(C1, 8, 4, 8, 8, 0.125 * 0.25)
    GC[NZC // 2, yc, pl.ds(gx, 1), :] = restrict_two(C2, 0.125 * 0.25)
    start_z(GC, cg)

    for copy in e0c:
        copy.wait_recv()
    coefficients(C0, CX0, CY0, CZ0, W0, 22)
    for copy in e0v + e0b:
        copy.wait_recv()
    zero = (B0, CX0, CY0, CZ0)
    sweep(V0, VA0, *zero, W0, 1, 21)
    sweep(VA0, VB0, *zero, W0, 2, 20)
    flux_loop(VB0, *zero, 3, 19, lambda x, v, r: put(VA0, x, r))
    B1[8:16, 8:16] = restrict_zero(VA0, 0.125)
    b1 = exchange(B1, (8, 8), 8, 6, b1s, b1r, 5)
    for copy in b1:
        copy.start()

    h0 = [
        remote(VB0.at[pl.ds(sx, nx), :, pl.ds(sy, ny), :], VH.at[pl.ds(tx, nx), :, pl.ds(ty, ny), :],
               h0s.at[i], h0r.at[i], beside(*o))
        for i, (o, (sx, tx, nx), (sy, ty, ny)) in enumerate((
            ((0, 1), (3, 3, 16), (18, 2, 1)),
            ((0, -1), (3, 3, 16), (5, 21, 1)),
            ((1, 0), (17, 1, 1), (4, 4, 16)),
            ((-1, 0), (4, 20, 1), (4, 4, 16)),
            ((1, 1), (18, 2, 1), (19, 3, 1)),
            ((1, -1), (18, 2, 1), (4, 20, 1)),
            ((-1, 1), (3, 19, 1), (19, 3, 1)),
            ((-1, -1), (3, 19, 1), (4, 20, 1)),
        ))
    ]
    for copy in h0:
        copy.start()

    landed_z(cg)
    start_plane(GC, cg)

    for copy in c1:
        copy.wait_recv()
    coefficients(C1, CX1, CY1, CZ1, W1, 24)
    for k in range(3):
        C2[4 * k : 4 * k + 4, 0:12] = restrict_one(C1, 8 * k, 4, 0, 24, 0.125 * 0.25)
    coefficients(C2, CX2, CY2, CZ2, W2, 12)

    for copy in b1:
        copy.wait_recv()

    def from_zero(to_ref, b_ref, w_ref, lo, hi):
        to_ref[lo:hi] = w_ref[lo:hi] * b_ref[lo:hi]

    one = (B1, CX1, CY1, CZ1)
    from_zero(VA1, B1, W1, 2, 22)
    sweep(VA1, VB1, *one, W1, 3, 21)
    flux_loop(VB1, *one, 4, 20, lambda x, v, r: put(R1, x, r))
    B2[2:10, 0:12] = restrict_one(R1, 4, 8, 0, 24, 0.125)

    two = (B2, CX2, CY2, CZ2)
    from_zero(VA2, B2, W2, 2, 10)
    sweep(VA2, VB2, *two, W2, 3, 9)
    flux_loop(VB2, *two, 4, 8, lambda x, v, r: put(R2, x, r))
    GB[NZC // 2, yc, pl.ds(gx, 1), :] = restrict_two(R2, 0.125)
    start_z(GB, bg)
    B2H[4:8, 4:8] = B2[4:8, 4:8]
    V2H[4:8, 4:8] = VB2[4:8, 4:8]
    h2 = exchange(B2H, (4, 4), 4, 4, h2s.at[0], h2r.at[0]) + exchange(V2H, (4, 4), 4, 4, h2s.at[1], h2r.at[1])
    for copy in h2:
        copy.start()

    landed_plane(cg)
    C3[1 : GY + 1] = GC[...].reshape(GY, GX, 128)
    wrap_rows(C3)
    whole_coefficients(THREE, C3, K3)
    C4[1 : GY + 1] = coarsen_lanes(C3[1 : GY + 1]) * (0.125 * 0.25)
    wrap_rows(C4)
    whole_coefficients(FOUR, C4, K4)

    landed_z(bg)
    start_plane(GB, bg)
    landed_plane(bg)

    b3 = GB[...].reshape(GY, GX, 128)
    B3[1 : GY + 1] = b3
    V3A[1 : GY + 1] = K3[7] * b3
    wrap_rows(V3A)
    whole_sweep(THREE, V3A, V3B, B3, K3)

    def residual(lo, hi, v, s):
        r = B3[lo + 1 : hi + 1] + s - K3[6, lo:hi] * v
        B4[lo + 1 : hi + 1] = coarsen_lanes(r) * 0.125

    whole_sum(THREE, V3B, K3, residual, 0, GY)

    b4 = B4[1 : GY + 1]
    b4 = b4 - jnp.sum(jnp.sum(b4, axis=0), keepdims=True) * (1.0 / (GY * GX * 128))
    B4[1 : GY + 1] = b4
    V4A[7:31] = K4[7, 6:30] * b4[6:30]
    here, there = V4A, V4B
    for i in range(7):
        whole_sweep(FOUR, here, there, B4, K4, 7 + i, 29 - i)
        here, there = there, here

    V3B[14:24] = V3B[14:24] + here[14:24]
    whole_sweep(THREE, V3B, V3A, B3, K3, 14, 22)
    whole_sweep(THREE, V3A, V3B, B3, K3, 15, 21)

    near = [
        pltpu.roll(V3B[4 * (NZC // 2) + yc + j], lax.rem(1 - gx + GX, GX), 0) for j in range(3)
    ]
    u = mm(jnp.concatenate(near, axis=0), MP3[...])
    for copy in h2:
        copy.wait_recv()
    pair = lax.broadcasted_iota(jnp.int32, (16, 128), 0) // 2
    for x3 in range(6):
        i, dx = x3 // 2, x3 % 2
        rise = jnp.zeros((16, 128), F32)
        for y3 in range(6):
            j, g = y3 // 2, 2 * dx + y3 % 2
            rise = jnp.where(pair == y3, u[8 * j + i : 8 * j + i + 1, 128 * g : 128 * g + 128], rise)
        for x in (2 * x3, 2 * x3 + 1):
            VA2[x] = V2H[x] + rise
    two = (B2H, CX2, CY2, CZ2)
    sweep(VA2, R2, *two, W2, 1, 11)
    sweep(R2, VA2, *two, W2, 2, 10)

    for k in range(8):
        rows = VA2[2 + k, 0:12, :]
        TP1[k, pl.ds(0, 12, stride=2), :] = rows
        TP1[k, pl.ds(1, 12, stride=2), :] = rows
    TR[0:8] = mm(TP1[...].reshape(8 * 24, 128), MP2[...]).reshape(8, 24, 128)
    for x in range(5, 19):
        VA1[x] = VB1[x] + TR[x // 2 - 2]
    sweep(VA1, R1, *one, W1, 6, 18)
    sweep(R1, VA1, *one, W1, 7, 17)

    for k in range(10):
        rows = VA1[7 + k, 7:17, :]
        TP0[k, pl.ds(2, 10, stride=2), :] = rows
        TP0[k, pl.ds(3, 10, stride=2), :] = rows
    u = mm(TP0[...].reshape(10 * 24, 128), MP1[...])
    for h in range(2):
        PE0[:, h] = u[:, 128 * h : 128 * h + 128].reshape(10, 24, 128)
    for copy in h0:
        copy.wait_recv()
    row = lax.broadcasted_iota(jnp.int32, (24, 128), 0)
    outer = (row == 2) | (row == 21)

    def raise_slab(x, carry):
        for h in range(2):
            VA0[x, h] = jnp.where(outer, VH[x, h], VB0[x, h]) + PE0[lax.div(x - 1, 2), h]
        return carry

    lax.fori_loop(3, 19, raise_slab, 0, unroll=8)
    corner = (row == 3) | (row == 20)
    for h in range(2):
        for x in (1, 20):
            VA0[x, h] = VH[x, h] + PE0[(x - 1) // 2, h]
        for x in (2, 19):
            VA0[x, h] = jnp.where(corner, VH[x, h], VB0[x, h]) + PE0[(x - 1) // 2, h]
    for copy in e0c + e0v + e0b:
        copy.wait_send()
    sweep(VA0, V0, *zero, W0, 2, 20)

    def last(x, v, r):
        s = add(v, mul(get(W0, x), r))
        for h in range(2):
            out_ref[x - 3, :, 128 * h : 128 * h + 128] = s[h][4:20]

    flux_loop(V0, *zero, 3, 19, last)

    for copy in c1 + b1 + h0 + h2:
        copy.wait_send()
    sent(cg)
    sent(bg)


def solution(mesh):
    def vmem(*shape):
        return pltpu.VMEM(shape, F32)

    def half(*shape):
        return pltpu.VMEM(shape, BF16)

    dma = pltpu.SemaphoreType.DMA
    scratch = (
        [vmem(22, 2, 24, 128)] * 10
        + [vmem(8, 24, 128), vmem(10, 2, 24, 128), vmem(10, 24, 128)]
        + [vmem(24, 24, 128)] * 9
        + [vmem(8, 24, 128)]
        + [vmem(12, 16, 128)] * 11
        + [vmem(GY + 2, GX, 128)] * 4
        + [vmem(8, GY, GX, 128)]
        + [vmem(GY + 2, GX, 128)] * 4
        + [vmem(8, GY, GX, 128)]
        + [vmem(NZC, NYC, GX, 128)] * 2
        + [half(384, 128), half(128, 128), half(128, 256), half(128, 128), half(128, 512)]
        + [vmem(GX * NYC - 1, NZC, 128)]
        + [dma((6,)), dma((3, 8)), dma((3, 8))]
        + [dma((8,))] * 6
        + [dma((2, 8))] * 2
        + [dma((4,))] * 2
    )

    def step(source, conductivity, guess):
        return pl.pallas_call(
            kernel,
            out_shape=jax.ShapeDtypeStruct(source.shape, F32),
            in_specs=[pl.BlockSpec(memory_space=pl.ANY)] * 3,
            out_specs=pl.BlockSpec(memory_space=pltpu.VMEM),
            scratch_shapes=scratch,
            compiler_params=pltpu.CompilerParams(
                collective_id=0, has_side_effects=True, vmem_limit_bytes=54848 * 2**10
            ),
            name="vcycle",
        )(source, conductivity, guess)

    spec = P("gx", "gy", None)
    return jax.shard_map(step, mesh=mesh, in_specs=(spec, spec, spec), out_specs=spec, check_vma=False)
```

```python
import jax
import jax.numpy as jnp
from jax import lax
from jax.experimental import pallas as pl
from jax.experimental.pallas import tpu as pltpu
from jax.sharding import PartitionSpec as P

MESH = pl.DeviceIdType.MESH
F32, BF16 = jnp.float32, jnp.bfloat16
OMEGA = 0.8
GX, GY, NYC, NZC = 8, 32, 4, 8
FAR_FIRST = sorted(
    ((dx, dy) for dx in range(GX) for dy in range(NYC) if dx or dy),
    key=lambda o: -(min(o[0], GX - o[0]) + 2 * min(o[1], NYC - o[1])),
)
EIGHT = [(1, 1), (1, -1), (-1, 1), (-1, -1), (0, 1), (0, -1), (1, 0), (-1, 0)]


def harmonic(a, b):
    return 2.0 * a * b / (a + b)


def mm(a, m):
    hi = a.astype(BF16)
    lo = (a - hi.astype(F32)).astype(BF16)
    return jnp.dot(jnp.concatenate([hi, lo], axis=1), m, preferred_element_type=F32)


def zp(s):
    if len(s) == 1:
        return (pltpu.roll(s[0], 126 if s[0].shape[0] == 16 else 127, 1),)
    last = lax.broadcasted_iota(jnp.int32, s[0].shape, 1) == 127
    a, b = pltpu.roll(s[0], 127, 1), pltpu.roll(s[1], 127, 1)
    return (jnp.where(last, b, a), jnp.where(last, a, b))


def zm(s):
    if len(s) == 1:
        return (pltpu.roll(s[0], 2 if s[0].shape[0] == 16 else 1, 1),)
    first = lax.broadcasted_iota(jnp.int32, s[0].shape, 1) == 0
    a, b = pltpu.roll(s[0], 1, 1), pltpu.roll(s[1], 1, 1)
    return (jnp.where(first, b, a), jnp.where(first, a, b))


def yp(s):
    return tuple(pltpu.roll(a, a.shape[0] - 1, 0) for a in s)


def ym(s):
    return tuple(pltpu.roll(a, 1, 0) for a in s)


def each(f, *slabs):
    return tuple(f(*a) for a in zip(*slabs))


def get(ref, x):
    if len(ref.shape) == 4:
        return (ref[x, 0], ref[x, 1])
    return (ref[x],)


def put(ref, x, s):
    if len(ref.shape) == 4:
        ref[x, 0] = s[0]
        ref[x, 1] = s[1]
    else:
        ref[x] = s[0]


def add(a, b):
    return each(lambda p, q: p + q, a, b)


def sub(a, b):
    return each(lambda p, q: p - q, a, b)


def mul(a, b):
    return each(lambda p, q: p * q, a, b)


def steps_of(count, most):
    return max(n for n in range(1, most + 1) if count % n == 0)


def coefficients(c_ref, cx_ref, cy_ref, cz_ref, w_ref, slabs):
    c = get(c_ref, 0)
    n = get(c_ref, 1)
    first = each(harmonic, c, n)
    put(cx_ref, 0, first)

    def body(x, carry):
        c, before = carry
        n = get(c_ref, x + 1)
        ex = each(harmonic, c, n)
        ey = each(harmonic, c, yp(c))
        ez = each(harmonic, c, zp(c))
        d = add(add(add(ex, before), add(ey, ym(ey))), add(ez, zm(ez)))
        put(cx_ref, x, ex)
        put(cy_ref, x, ey)
        put(cz_ref, x, ez)
        put(w_ref, x, each(lambda p: OMEGA / p, d))
        return n, ex

    lax.fori_loop(1, slabs - 1, body, (n, first), unroll=steps_of(slabs - 2, UNROLL_FACES[len(c_ref.shape)]))


def flux_loop(v_ref, b_ref, cx_ref, cy_ref, cz_ref, lo, hi, emit):
    v = get(v_ref, lo)
    before = mul(get(cx_ref, lo - 1), sub(v, get(v_ref, lo - 1)))

    def body(x, carry):
        v, before = carry
        n = get(v_ref, x + 1)
        tx = mul(get(cx_ref, x), sub(n, v))
        ty = mul(get(cy_ref, x), sub(yp(v), v))
        tz = mul(get(cz_ref, x), sub(zp(v), v))
        r = add(add(sub(tx, before), sub(ty, ym(ty))), sub(tz, zm(tz)))
        emit(x, v, add(get(b_ref, x), r))
        return n, tx

    lax.fori_loop(lo, hi, body, (v, before), unroll=steps_of(hi - lo, UNROLL[len(v_ref.shape)]))


def sweep(v_ref, to_ref, b_ref, cx_ref, cy_ref, cz_ref, w_ref, lo, hi):
    def emit(x, v, r):
        put(to_ref, x, add(v, mul(get(w_ref, x), r)))

    flux_loop(v_ref, b_ref, cx_ref, cy_ref, cz_ref, lo, hi, emit)


def lane(shape):
    return lax.broadcasted_iota(jnp.int32, shape, len(shape) - 1)


def three_zp(v):
    return jnp.where(lane(v.shape) % 32 == 31, pltpu.roll(v, 31, 2), pltpu.roll(v, 127, 2))


def three_zm(v):
    return jnp.where(lane(v.shape) % 32 == 0, pltpu.roll(v, 97, 2), pltpu.roll(v, 1, 2))


def three_xp(v):
    r = pltpu.roll(v, 64, 2)
    return jnp.where(lane(v.shape) < 64, r, pltpu.roll(r, GX - 1, 1))


def three_xm(v):
    r = pltpu.roll(v, 64, 2)
    return jnp.where(lane(v.shape) < 64, pltpu.roll(r, 1, 1), r)


def three_y(v):
    up, down = pltpu.roll(v, 96, 2), pltpu.roll(v, 32, 2)
    first = lane(v[1:-1].shape) % 64 < 32
    return (jnp.where(first, up[1:-1], down[2:]), jnp.where(first, up[:-2], down[1:-1]))


def four_zp(v):
    return pltpu.roll(v, 126, 2)


def four_zm(v):
    return pltpu.roll(v, 2, 2)


def four_xp(v):
    return pltpu.roll(v, GX - 1, 1)


def four_xm(v):
    return pltpu.roll(v, 1, 1)


def four_y(v):
    return v[2:], v[:-2]


THREE = (three_xp, three_xm, three_y, three_zp, three_zm)
FOUR = (four_xp, four_xm, four_y, four_zp, four_zm)
UNROLL = {4: 10, 3: 20}
UNROLL_FACES = {4: 10, 3: 11}


def wrap_rows(ref):
    ref[0] = ref[GY]
    ref[GY + 1] = ref[1]


def chunks(lo, hi):
    parts = -(-(hi - lo) // 16)
    cuts = [lo + (hi - lo) * i // parts for i in range(parts + 1)]
    return list(zip(cuts[:-1], cuts[1:]))


def whole_coefficients(level, c_ref, k_ref):
    xp, xm, y, zplus, zminus = level
    for lo, hi in chunks(0, GY):
        ext = c_ref[lo : hi + 2]
        c = ext[1:-1]
        up, down = y(ext)
        ex = harmonic(c, xp(c))
        ez = harmonic(c, zplus(c))
        ey, wy = harmonic(c, up), harmonic(down, c)
        wx, wz = xm(ex), zminus(ez)
        d = (ex + wx) + (ey + wy) + (ez + wz)
        for j, value in enumerate((ex, wx, ey, wy, ez, wz, d, OMEGA / d)):
            k_ref[j, lo:hi] = value


def whole_sum(level, v_ref, k_ref, emit, first, last):
    xp, xm, y, zplus, zminus = level
    for lo, hi in chunks(first, last):
        ext = v_ref[lo : hi + 2]
        v = ext[1:-1]
        up, down = y(ext)
        k = [k_ref[j, lo:hi] for j in range(6)]
        s = (k[0] * xp(v) + k[1] * xm(v)) + (k[2] * up + k[3] * down)
        emit(lo, hi, v, s + (k[4] * zplus(v) + k[5] * zminus(v)))


def whole_sweep(level, v_ref, to_ref, b_ref, k_ref, first=0, last=GY):
    def emit(lo, hi, v, s):
        to_ref[lo + 1 : hi + 1] = (1.0 - OMEGA) * v + k_ref[7, lo:hi] * (b_ref[lo + 1 : hi + 1] + s)

    whole_sum(level, v_ref, k_ref, emit, first, last)
    if last - first == GY:
        wrap_rows(to_ref)


def coarsen_lanes(v):
    s = v + pltpu.roll(v, 64, 2)
    s = s + pltpu.roll(s, 32, 2)
    return s + jnp.where(lane(v.shape) % 2 == 0, pltpu.roll(s, 127, 2), pltpu.roll(s, 1, 2))


def kernel(
    src_ref, cond_ref, guess_ref, out_ref,
    V0, B0, C0, CX0, CY0, CZ0, W0, VA0, VB0, VH, TR, PE0, TP0,
    C1, CX1, CY1, CZ1, W1, B1, VA1, VB1, R1, TP1,
    C2, CX2, CY2, CZ2, W2, B2, VA2, VB2, R2, B2H, V2H,
    C3, B3, V3A, V3B, K3, C4, B4, V4A, V4B, K4, GC, GB,
    MR, M3, MP1, MP3, ROWS,
    lsem, e0s, e0r, c1s, c1r, b1s, b1r, h0s, h0r, h2s, h2r, cg, bg,
):
    gx, gy = lax.axis_index("gx"), lax.axis_index("gy")
    yc, zc = lax.rem(gy, NYC), lax.div(gy, NYC)

    def beside(dx, dy):
        return (lax.rem(gx + dx + GX, GX), lax.rem(gy + dy + GY, GY))

    def in_plane(k):
        return (lax.rem(gx + lax.div(k, NYC), GX), zc * NYC + lax.rem(yc + lax.rem(k, NYC), NYC))

    def along_z(k):
        return (gx, lax.rem(zc + k, NZC) * NYC + yc)

    def remote(src, dst, send, recv, device):
        return pltpu.make_async_remote_copy(
            src_ref=src, dst_ref=dst, send_sem=send, recv_sem=recv, device_id=device, device_id_type=MESH
        )

    loads = []
    for i, (ref, to) in enumerate(((cond_ref, C0), (guess_ref, V0), (src_ref, B0))):
        for h in range(2):
            loads.append(
                pltpu.make_async_copy(
                    ref.at[:, :, pl.ds(128 * h, 128)],
                    to.at[pl.ds(3, 16), h, pl.ds(4, 16), :],
                    lsem.at[2 * i + h],
                )
            )
    for copy in loads:
        copy.start()

    barrier = pltpu.get_barrier_semaphore()
    for dx, dy in EIGHT:
        pl.semaphore_signal(barrier, inc=1, device_id=beside(dx, dy), device_id_type=MESH)

    def greet_plane(k, carry):
        pl.semaphore_signal(barrier, inc=1, device_id=in_plane(k), device_id_type=MESH)
        return carry

    def greet_z(k, carry):
        pl.semaphore_signal(barrier, inc=1, device_id=along_z(k), device_id_type=MESH)
        return carry

    lax.fori_loop(1, NZC, greet_z, 0)
    lax.fori_loop(1, GX * NYC, greet_plane, 0)

    pl.semaphore_wait(barrier, len(EIGHT) + GX * NYC - 1 + NZC - 1)

    def edge(base, extent, step, width):
        if step == 0:
            return base, base, extent
        if step == 1:
            return base + extent - width, base - width, width
        return base, base + extent, width

    def block_copy(ref, base, extent, step, width, send, recv):
        sx, tx, nx = edge(base[0], extent, step[0], width)
        sy, ty, ny = edge(base[1], extent, step[1], width)
        if len(ref.shape) == 4:
            src, dst = ref.at[pl.ds(sx, nx), :, pl.ds(sy, ny), :], ref.at[pl.ds(tx, nx), :, pl.ds(ty, ny), :]
        else:
            src, dst = ref.at[pl.ds(sx, nx), pl.ds(sy, ny), :], ref.at[pl.ds(tx, nx), pl.ds(ty, ny), :]
        return remote(src, dst, send, recv, beside(*step))

    def exchange(ref, base, extent, width, send, recv, corner=None):
        return [
            block_copy(ref, base, extent, o, corner if corner and o[0] and o[1] else width, send.at[i], recv.at[i])
            for i, o in enumerate(EIGHT)
        ]

    e0c = exchange(C0, (3, 4), 16, 3, e0s.at[0], e0r.at[0], 2)
    e0v = exchange(V0, (3, 4), 16, 3, e0s.at[1], e0r.at[1], 2)
    e0b = exchange(B0, (3, 4), 16, 2, e0s.at[2], e0r.at[2], 1)
    for first in (0, 4, 6):
        for n, copies in enumerate((e0c, e0v, e0b)):
            if first == 0:
                loads[2 * n].wait()
                loads[2 * n + 1].wait()
            for copy in copies[first : first + 4 if first == 0 else first + 2]:
                copy.start()

    def matrix(rows, columns, rule):
        r = lax.broadcasted_iota(jnp.int32, (2 * rows, columns), 0) % rows
        c = lax.broadcasted_iota(jnp.int32, (2 * rows, columns), 1)
        return jnp.where(rule(r, c), 1.0, 0.0).astype(BF16)

    MR[...] = matrix(256, 128, lambda r, c: r // 2 == c)
    M3[...] = matrix(128, 128, lambda r, c: (r % 2 == 0) & (r // 4 == c % 32))
    MP1[...] = matrix(128, 256, lambda r, c: r == c // 2)
    MP3[...] = matrix(128, 512, lambda r, c: (r // 32 == c // 128) & (r % 32 == (c % 128) // 4))

    def restrict_zero(ref, scale):
        pairs = [
            jnp.concatenate([ref[3 + 2 * k, h, 4:20] + ref[4 + 2 * k, h, 4:20] for h in range(2)], axis=1)
            for k in range(8)
        ]
        TR[0:8, 0:16] = mm(jnp.concatenate(pairs, axis=0), MR[...]).reshape(8, 16, 128)
        return (TR[0:8, pl.ds(0, 8, stride=2), :] + TR[0:8, pl.ds(1, 8, stride=2), :]) * scale

    def restrict_one(ref, x0, count, y0, rows, scale):
        for k in range(count):
            TR[k, 0:rows] = ref[x0 + 2 * k, y0 : y0 + rows] + ref[x0 + 1 + 2 * k, y0 : y0 + rows]
        half = rows // 2
        s = (TR[0:count, pl.ds(0, half, stride=2), :] + TR[0:count, pl.ds(1, half, stride=2), :]) * scale
        return s + jnp.where(lane(s.shape) % 2 == 0, pltpu.roll(s, 127, 2), pltpu.roll(s, 1, 2))

    def restrict_two(ref, scale):
        pairs = jnp.concatenate([ref[4] + ref[5], ref[6] + ref[7]], axis=0)
        s = mm(pairs, M3[...]) * scale
        group = lax.broadcasted_iota(jnp.int32, (1, 128), 1) // 32
        row = jnp.zeros((1, 128), F32)
        for g in range(4):
            at = 16 * (g // 2) + 4 + 2 * (g % 2)
            row = jnp.where(group == g, s[at : at + 1] + s[at + 1 : at + 2], row)
        return row

    def z_copy(ref, k, sems):
        src = ref.at[NZC // 2, yc, pl.ds(gx, 1), :]
        dst = ref.at[(NZC // 2 - k) % NZC, yc, pl.ds(gx, 1), :]
        return remote(src, dst, sems.at[0], sems.at[1], along_z(k))

    def plane_copy(ref, dx, dy, sems):
        part = ref.at[:, yc, pl.ds(gx, 1), :]
        return remote(part, part, sems.at[2], sems.at[3], in_plane(dx * NYC + dy))

    def start_z(ref, sems):
        for k in (4, 3, 5, 2, 6, 1, 7):
            z_copy(ref, k, sems).start()

    def start_plane(ref, sems):
        for dx, dy in FAR_FIRST:
            plane_copy(ref, dx, dy, sems).start()

    def all_bytes(kind, sem):
        part = ROWS.at[0, pl.ds(0, NZC - 1), :] if kind == 0 else ROWS
        pltpu.make_async_copy(part, part, sem).wait()

    def landed_z(sems):
        all_bytes(0, sems.at[1])

    def landed_plane(sems):
        all_bytes(1, sems.at[3])

    def sent(sems):
        all_bytes(0, sems.at[0])
        all_bytes(1, sems.at[2])

    C1[8:16, 8:16] = restrict_zero(C0, 0.125 * 0.25)
    c1 = exchange(C1, (8, 8), 8, 8, c1s, c1r)
    C2[4:8, 4:8] = restrict_one(C1, 8, 4, 8, 8, 0.125 * 0.25)
    GC[NZC // 2, yc, pl.ds(gx, 1), :] = restrict_two(C2, 0.125 * 0.25)
    start_z(GC, cg)

    for copy in e0c:
        copy.wait_recv()
    for copy in c1:
        copy.start()
    coefficients(C0, CX0, CY0, CZ0, W0, 22)
    for copy in e0v + e0b:
        copy.wait_recv()
    zero = (B0, CX0, CY0, CZ0)
    sweep(V0, VA0, *zero, W0, 1, 21)
    sweep(VA0, VB0, *zero, W0, 2, 20)
    flux_loop(VB0, *zero, 3, 19, lambda x, v, r: put(VA0, x, r))
    B1[8:16, 8:16] = restrict_zero(VA0, 0.125)
    b1 = exchange(B1, (8, 8), 8, 6, b1s, b1r, 5)
    for copy in b1:
        copy.start()

    h0 = [
        remote(VB0.at[pl.ds(sx, nx), :, pl.ds(sy, ny), :], VH.at[pl.ds(tx, nx), :, pl.ds(ty, ny), :],
               h0s.at[i], h0r.at[i], beside(*o))
        for i, (o, (sx, tx, nx), (sy, ty, ny)) in enumerate((
            ((0, 1), (3, 3, 16), (18, 2, 1)),
            ((0, -1), (3, 3, 16), (5, 21, 1)),
            ((1, 0), (17, 1, 1), (4, 4, 16)),
            ((-1, 0), (4, 20, 1), (4, 4, 16)),
            ((1, 1), (18, 2, 1), (19, 3, 1)),
            ((1, -1), (18, 2, 1), (4, 20, 1)),
            ((-1, 1), (3, 19, 1), (19, 3, 1)),
            ((-1, -1), (3, 19, 1), (4, 20, 1)),
        ))
    ]
    for copy in h0:
        copy.start()

    landed_z(cg)
    start_plane(GC, cg)

    for copy in c1:
        copy.wait_recv()
    coefficients(C1, CX1, CY1, CZ1, W1, 24)
    for k in range(3):
        C2[4 * k : 4 * k + 4, 0:12] = restrict_one(C1, 8 * k, 4, 0, 24, 0.125 * 0.25)
    coefficients(C2, CX2, CY2, CZ2, W2, 12)

    for copy in b1:
        copy.wait_recv()

    def from_zero(to_ref, b_ref, w_ref, lo, hi):
        to_ref[lo:hi] = w_ref[lo:hi] * b_ref[lo:hi]

    one = (B1, CX1, CY1, CZ1)
    from_zero(VA1, B1, W1, 2, 22)
    sweep(VA1, VB1, *one, W1, 3, 21)
    flux_loop(VB1, *one, 4, 20, lambda x, v, r: put(R1, x, r))
    B2[2:10, 0:12] = restrict_one(R1, 4, 8, 0, 24, 0.125)

    two = (B2, CX2, CY2, CZ2)
    from_zero(VA2, B2, W2, 2, 10)
    sweep(VA2, VB2, *two, W2, 3, 9)
    flux_loop(VB2, *two, 4, 8, lambda x, v, r: put(R2, x, r))
    GB[NZC // 2, yc, pl.ds(gx, 1), :] = restrict_two(R2, 0.125)
    start_z(GB, bg)
    B2H[4:8, 4:8] = B2[4:8, 4:8]
    V2H[4:8, 4:8] = VB2[4:8, 4:8]
    h2 = exchange(B2H, (4, 4), 4, 4, h2s.at[0], h2r.at[0]) + exchange(V2H, (4, 4), 4, 4, h2s.at[1], h2r.at[1])
    for copy in h2:
        copy.start()

    landed_plane(cg)
    C3[1 : GY + 1] = GC[...].reshape(GY, GX, 128)
    wrap_rows(C3)
    whole_coefficients(THREE, C3, K3)
    C4[1 : GY + 1] = coarsen_lanes(C3[1 : GY + 1]) * (0.125 * 0.25)
    wrap_rows(C4)
    whole_coefficients(FOUR, C4, K4)

    landed_z(bg)
    start_plane(GB, bg)
    landed_plane(bg)

    b3 = GB[...].reshape(GY, GX, 128)
    B3[1 : GY + 1] = b3
    V3A[1 : GY + 1] = K3[7] * b3
    wrap_rows(V3A)
    whole_sweep(THREE, V3A, V3B, B3, K3)

    def residual(lo, hi, v, s):
        r = B3[lo + 1 : hi + 1] + s - K3[6, lo:hi] * v
        B4[lo + 1 : hi + 1] = coarsen_lanes(r) * 0.125

    whole_sum(THREE, V3B, K3, residual, 0, GY)

    b4 = B4[1 : GY + 1]
    b4 = b4 - jnp.sum(jnp.sum(b4, axis=0), keepdims=True) * (1.0 / (GY * GX * 128))
    B4[1 : GY + 1] = b4
    V4A[7:31] = K4[7, 6:30] * b4[6:30]
    here, there = V4A, V4B
    for i in range(7):
        whole_sweep(FOUR, here, there, B4, K4, 7 + i, 29 - i)
        here, there = there, here

    V3B[14:24] = V3B[14:24] + here[14:24]
    whole_sweep(THREE, V3B, V3A, B3, K3, 14, 22)
    whole_sweep(THREE, V3A, V3B, B3, K3, 15, 21)

    near = [
        pltpu.roll(V3B[4 * (NZC // 2) + yc + j], lax.rem(1 - gx + GX, GX), 0) for j in range(3)
    ]
    u = mm(jnp.concatenate(near, axis=0), MP3[...])
    for copy in h2:
        copy.wait_recv()
    pair = lax.broadcasted_iota(jnp.int32, (16, 128), 0) // 2
    for x3 in range(6):
        i, dx = x3 // 2, x3 % 2
        rise = jnp.zeros((16, 128), F32)
        for y3 in range(6):
            j, g = y3 // 2, 2 * dx + y3 % 2
            rise = jnp.where(pair == y3, u[8 * j + i : 8 * j + i + 1, 128 * g : 128 * g + 128], rise)
        for x in (2 * x3, 2 * x3 + 1):
            VA2[x] = V2H[x] + rise
    two = (B2H, CX2, CY2, CZ2)
    sweep(VA2, R2, *two, W2, 1, 11)
    sweep(R2, VA2, *two, W2, 2, 10)

    for k in range(8):
        rows = VA2[2 + k, 0:12, :]
        TP1[k, pl.ds(0, 12, stride=2), :] = rows
        TP1[k, pl.ds(1, 12, stride=2), :] = rows
    for x in range(5, 19):
        VA1[x] = VB1[x] + TP1[x // 2 - 2]
    sweep(VA1, R1, *one, W1, 6, 18)
    sweep(R1, VA1, *one, W1, 7, 17)

    for k in range(10):
        rows = VA1[7 + k, 7:17, :]
        TP0[k, pl.ds(2, 10, stride=2), :] = rows
        TP0[k, pl.ds(3, 10, stride=2), :] = rows
    u = mm(TP0[...].reshape(10 * 24, 128), MP1[...])
    for h in range(2):
        PE0[:, h] = u[:, 128 * h : 128 * h + 128].reshape(10, 24, 128)
    for copy in h0:
        copy.wait_recv()
    row = lax.broadcasted_iota(jnp.int32, (24, 128), 0)
    outer = (row == 2) | (row == 21)

    def raise_slab(x, carry):
        for h in range(2):
            VA0[x, h] = jnp.where(outer, VH[x, h], VB0[x, h]) + PE0[lax.div(x - 1, 2), h]
        return carry

    lax.fori_loop(3, 19, raise_slab, 0, unroll=8)
    corner = (row == 3) | (row == 20)
    for h in range(2):
        for x in (1, 20):
            VA0[x, h] = VH[x, h] + PE0[(x - 1) // 2, h]
        for x in (2, 19):
            VA0[x, h] = jnp.where(corner, VH[x, h], VB0[x, h]) + PE0[(x - 1) // 2, h]
    for copy in e0c + e0v + e0b:
        copy.wait_send()
    sweep(VA0, V0, *zero, W0, 2, 20)

    def last(x, v, r):
        s = add(v, mul(get(W0, x), r))
        for h in range(2):
            out_ref[x - 3, :, 128 * h : 128 * h + 128] = s[h][4:20]

    flux_loop(V0, *zero, 3, 19, last)

    for copy in c1 + b1 + h0 + h2:
        copy.wait_send()
    sent(cg)
    sent(bg)


def solution(mesh):
    def vmem(*shape):
        return pltpu.VMEM(shape, F32)

    def half(*shape):
        return pltpu.VMEM(shape, BF16)

    dma = pltpu.SemaphoreType.DMA
    scratch = (
        [vmem(22, 2, 24, 128)] * 10
        + [vmem(8, 24, 128), vmem(10, 2, 24, 128), vmem(10, 24, 128)]
        + [vmem(24, 24, 128)] * 9
        + [vmem(8, 24, 128)]
        + [vmem(12, 16, 128)] * 11
        + [vmem(GY + 2, GX, 128)] * 4
        + [vmem(8, GY, GX, 128)]
        + [vmem(GY + 2, GX, 128)] * 4
        + [vmem(8, GY, GX, 128)]
        + [vmem(NZC, NYC, GX, 128)] * 2
        + [half(512, 128), half(256, 128), half(256, 256), half(256, 512)]
        + [vmem(GX * NYC - 1, NZC, 128)]
        + [dma((6,)), dma((3, 8)), dma((3, 8))]
        + [dma((8,))] * 6
        + [dma((2, 8))] * 2
        + [dma((4,))] * 2
    )

    def step(source, conductivity, guess):
        return pl.pallas_call(
            kernel,
            out_shape=jax.ShapeDtypeStruct(source.shape, F32),
            in_specs=[pl.BlockSpec(memory_space=pl.ANY)] * 3,
            out_specs=pl.BlockSpec(memory_space=pltpu.VMEM),
            scratch_shapes=scratch,
            compiler_params=pltpu.CompilerParams(
                collective_id=0, has_side_effects=True, vmem_limit_bytes=54848 * 2**10
            ),
            name="vcycle",
        )(source, conductivity, guess)

    spec = P("gx", "gy", None)
    return jax.shard_map(step, mesh=mesh, in_specs=(spec, spec, spec), out_specs=spec, check_vma=False)
```

```python
import jax
import jax.numpy as jnp
from jax import lax
from jax.experimental import pallas as pl
from jax.experimental.pallas import tpu as pltpu
from jax.sharding import PartitionSpec as P

MESH = pl.DeviceIdType.MESH
F32, BF16 = jnp.float32, jnp.bfloat16
OMEGA = 0.8
GX, GY, NYC, NZC = 8, 32, 4, 8
FAR_FIRST = sorted(
    ((dx, dy) for dx in range(GX) for dy in range(NYC) if dx or dy),
    key=lambda o: -(min(o[0], GX - o[0]) + 2 * min(o[1], NYC - o[1])),
)
EIGHT = [(1, 1), (1, -1), (-1, 1), (-1, -1), (0, 1), (0, -1), (1, 0), (-1, 0)]
Z_FAR_FIRST = (4, 3, 5, 2, 6, 1, 7)


def harmonic(a, b):
    return 2.0 * a * b / (a + b)


def mm(a, m):
    hi = a.astype(BF16)
    lo = (a - hi.astype(F32)).astype(BF16)
    return jnp.dot(jnp.concatenate([hi, lo], axis=1), m, preferred_element_type=F32)


def zp(s):
    if len(s) == 1:
        return (pltpu.roll(s[0], 126 if s[0].shape[0] == 16 else 127, 1),)
    last = lax.broadcasted_iota(jnp.int32, s[0].shape, 1) == 127
    a, b = pltpu.roll(s[0], 127, 1), pltpu.roll(s[1], 127, 1)
    return (jnp.where(last, b, a), jnp.where(last, a, b))


def zm(s):
    if len(s) == 1:
        return (pltpu.roll(s[0], 2 if s[0].shape[0] == 16 else 1, 1),)
    first = lax.broadcasted_iota(jnp.int32, s[0].shape, 1) == 0
    a, b = pltpu.roll(s[0], 1, 1), pltpu.roll(s[1], 1, 1)
    return (jnp.where(first, b, a), jnp.where(first, a, b))


def yp(s):
    return tuple(pltpu.roll(a, a.shape[0] - 1, 0) for a in s)


def ym(s):
    return tuple(pltpu.roll(a, 1, 0) for a in s)


def each(f, *slabs):
    return tuple(f(*a) for a in zip(*slabs))


def get(ref, x):
    if len(ref.shape) == 4:
        return (ref[x, 0], ref[x, 1])
    return (ref[x],)


def put(ref, x, s):
    if len(ref.shape) == 4:
        ref[x, 0] = s[0]
        ref[x, 1] = s[1]
    else:
        ref[x] = s[0]


def add(a, b):
    return each(lambda p, q: p + q, a, b)


def sub(a, b):
    return each(lambda p, q: p - q, a, b)


def mul(a, b):
    return each(lambda p, q: p * q, a, b)


def steps_of(count, most):
    return max(n for n in range(1, most + 1) if count % n == 0)


def coefficients(c_ref, cx_ref, cy_ref, cz_ref, w_ref, slabs):
    c = get(c_ref, 0)
    n = get(c_ref, 1)
    first = each(harmonic, c, n)
    put(cx_ref, 0, first)

    def body(x, carry):
        c, before = carry
        n = get(c_ref, x + 1)
        ex = each(harmonic, c, n)
        ey = each(harmonic, c, yp(c))
        ez = each(harmonic, c, zp(c))
        d = add(add(add(ex, before), add(ey, ym(ey))), add(ez, zm(ez)))
        put(cx_ref, x, ex)
        put(cy_ref, x, ey)
        put(cz_ref, x, ez)
        put(w_ref, x, each(lambda p: OMEGA / p, d))
        return n, ex

    lax.fori_loop(1, slabs - 1, body, (n, first), unroll=steps_of(slabs - 2, UNROLL_FACES[len(c_ref.shape)]))


def flux_loop(v_ref, b_ref, cx_ref, cy_ref, cz_ref, lo, hi, emit):
    v = get(v_ref, lo)
    before = mul(get(cx_ref, lo - 1), sub(v, get(v_ref, lo - 1)))

    def body(x, carry):
        v, before = carry
        n = get(v_ref, x + 1)
        tx = mul(get(cx_ref, x), sub(n, v))
        ty = mul(get(cy_ref, x), sub(yp(v), v))
        tz = mul(get(cz_ref, x), sub(zp(v), v))
        r = add(add(sub(tx, before), sub(ty, ym(ty))), sub(tz, zm(tz)))
        emit(x, v, add(get(b_ref, x), r))
        return n, tx

    lax.fori_loop(lo, hi, body, (v, before), unroll=steps_of(hi - lo, UNROLL[len(v_ref.shape)]))


def sweep(v_ref, to_ref, b_ref, cx_ref, cy_ref, cz_ref, w_ref, lo, hi):
    def emit(x, v, r):
        put(to_ref, x, add(v, mul(get(w_ref, x), r)))

    flux_loop(v_ref, b_ref, cx_ref, cy_ref, cz_ref, lo, hi, emit)


def lane(shape):
    return lax.broadcasted_iota(jnp.int32, shape, len(shape) - 1)


def three_zp(v):
    return jnp.where(lane(v.shape) % 32 == 31, pltpu.roll(v, 31, 2), pltpu.roll(v, 127, 2))


def three_zm(v):
    return jnp.where(lane(v.shape) % 32 == 0, pltpu.roll(v, 97, 2), pltpu.roll(v, 1, 2))


def three_xp(v):
    r = pltpu.roll(v, 64, 2)
    return jnp.where(lane(v.shape) < 64, r, pltpu.roll(r, GX - 1, 1))


def three_xm(v):
    r = pltpu.roll(v, 64, 2)
    return jnp.where(lane(v.shape) < 64, pltpu.roll(r, 1, 1), r)


def three_y(v):
    up, down = pltpu.roll(v, 96, 2), pltpu.roll(v, 32, 2)
    first = lane(v[1:-1].shape) % 64 < 32
    return (jnp.where(first, up[1:-1], down[2:]), jnp.where(first, up[:-2], down[1:-1]))


def four_zp(v):
    return pltpu.roll(v, 126, 2)


def four_zm(v):
    return pltpu.roll(v, 2, 2)


def four_xp(v):
    return pltpu.roll(v, GX - 1, 1)


def four_xm(v):
    return pltpu.roll(v, 1, 1)


def four_y(v):
    return v[2:], v[:-2]


THREE = (three_xp, three_xm, three_y, three_zp, three_zm)
FOUR = (four_xp, four_xm, four_y, four_zp, four_zm)
UNROLL = {4: 10, 3: 20}
UNROLL_FACES = {4: 10, 3: 11}


def wrap_rows(ref):
    ref[0] = ref[GY]
    ref[GY + 1] = ref[1]


def chunks(lo, hi):
    parts = -(-(hi - lo) // 16)
    cuts = [lo + (hi - lo) * i // parts for i in range(parts + 1)]
    return list(zip(cuts[:-1], cuts[1:]))


def whole_coefficients(level, c_ref, k_ref):
    xp, xm, y, zplus, zminus = level
    for lo, hi in chunks(0, GY):
        ext = c_ref[lo : hi + 2]
        c = ext[1:-1]
        up, down = y(ext)
        ex = harmonic(c, xp(c))
        ez = harmonic(c, zplus(c))
        ey, wy = harmonic(c, up), harmonic(down, c)
        wx, wz = xm(ex), zminus(ez)
        d = (ex + wx) + (ey + wy) + (ez + wz)
        for j, value in enumerate((ex, wx, ey, wy, ez, wz, d, OMEGA / d)):
            k_ref[j, lo:hi] = value


def whole_sum(level, v_ref, k_ref, emit, first, last):
    xp, xm, y, zplus, zminus = level
    for lo, hi in chunks(first, last):
        ext = v_ref[lo : hi + 2]
        v = ext[1:-1]
        up, down = y(ext)
        k = [k_ref[j, lo:hi] for j in range(6)]
        s = (k[0] * xp(v) + k[1] * xm(v)) + (k[2] * up + k[3] * down)
        emit(lo, hi, v, s + (k[4] * zplus(v) + k[5] * zminus(v)))


def whole_sweep(level, v_ref, to_ref, b_ref, k_ref, first=0, last=GY):
    def emit(lo, hi, v, s):
        to_ref[lo + 1 : hi + 1] = (1.0 - OMEGA) * v + k_ref[7, lo:hi] * (b_ref[lo + 1 : hi + 1] + s)

    whole_sum(level, v_ref, k_ref, emit, first, last)
    if last - first == GY:
        wrap_rows(to_ref)


def coarsen_lanes(v):
    s = v + pltpu.roll(v, 64, 2)
    s = s + pltpu.roll(s, 32, 2)
    return s + jnp.where(lane(v.shape) % 2 == 0, pltpu.roll(s, 127, 2), pltpu.roll(s, 1, 2))


def kernel(
    src_ref, cond_ref, guess_ref, out_ref,
    V0, B0, C0, CX0, CY0, CZ0, W0, VA0, VB0, VH, TR, PE0, TP0,
    C1, CX1, CY1, CZ1, W1, B1, VA1, VB1, R1, TP1,
    C2, CX2, CY2, CZ2, W2, B2, VA2, VB2, R2, B2H, V2H,
    C3, B3, V3A, V3B, K3, C4, B4, V4A, V4B, K4, GC, GB,
    MR, M3, MP1, MP3, ROWS,
    lsem, e0s, e0r, c1s, c1r, b1s, b1r, h0s, h0r, h2s, h2r, cg, bg,
):
    gx, gy = lax.axis_index("gx"), lax.axis_index("gy")
    yc, zc = lax.rem(gy, NYC), lax.div(gy, NYC)

    def beside(dx, dy):
        return (lax.rem(gx + dx + GX, GX), lax.rem(gy + dy + GY, GY))

    def along_z(k):
        return (gx, lax.rem(zc + k, NZC) * NYC + yc)

    def remote(src, dst, send, recv, device):
        return pltpu.make_async_remote_copy(
            src_ref=src, dst_ref=dst, send_sem=send, recv_sem=recv, device_id=device, device_id_type=MESH
        )

    loads = []
    for i, (ref, to) in enumerate(((cond_ref, C0), (guess_ref, V0), (src_ref, B0))):
        for h in range(2):
            loads.append(
                pltpu.make_async_copy(
                    ref.at[:, :, pl.ds(128 * h, 128)],
                    to.at[pl.ds(3, 16), h, pl.ds(4, 16), :],
                    lsem.at[2 * i + h],
                )
            )
    barrier = pltpu.get_barrier_semaphore()
    for dx, dy in EIGHT:
        pl.semaphore_signal(barrier, inc=1, device_id=beside(dx, dy), device_id_type=MESH)

    columns = [lax.rem(gx + d, GX) for d in range(GX)]
    rows = [zc * NYC + lax.rem(yc + d, NYC) for d in range(NYC)]
    for dx, dy in FAR_FIRST:
        pl.semaphore_signal(barrier, inc=1, device_id=(columns[dx], rows[dy]), device_id_type=MESH)
    for k in Z_FAR_FIRST:
        pl.semaphore_signal(barrier, inc=1, device_id=along_z(k), device_id_type=MESH)
    for copy in loads:
        copy.start()

    pl.semaphore_wait(barrier, len(EIGHT) + GX * NYC - 1 + NZC - 1)

    def edge(base, extent, step, width):
        if step == 0:
            return base, base, extent
        if step == 1:
            return base + extent - width, base - width, width
        return base, base + extent, width

    def block_copy(ref, base, extent, step, width, send, recv):
        sx, tx, nx = edge(base[0], extent, step[0], width)
        sy, ty, ny = edge(base[1], extent, step[1], width)
        if len(ref.shape) == 4:
            src, dst = ref.at[pl.ds(sx, nx), :, pl.ds(sy, ny), :], ref.at[pl.ds(tx, nx), :, pl.ds(ty, ny), :]
        else:
            src, dst = ref.at[pl.ds(sx, nx), pl.ds(sy, ny), :], ref.at[pl.ds(tx, nx), pl.ds(ty, ny), :]
        return remote(src, dst, send, recv, beside(*step))

    def exchange(ref, base, extent, width, send, recv, corner=None):
        return [
            block_copy(ref, base, extent, o, corner if corner and o[0] and o[1] else width, send.at[i], recv.at[i])
            for i, o in enumerate(EIGHT)
        ]

    e0c = exchange(C0, (3, 4), 16, 3, e0s.at[0], e0r.at[0], 2)
    e0v = exchange(V0, (3, 4), 16, 3, e0s.at[1], e0r.at[1], 2)
    e0b = exchange(B0, (3, 4), 16, 2, e0s.at[2], e0r.at[2], 1)
    for first in (0, 4, 6):
        for n, copies in enumerate((e0c, e0v, e0b)):
            if first == 0:
                loads[2 * n].wait()
                loads[2 * n + 1].wait()
            for copy in copies[first : first + 4 if first == 0 else first + 2]:
                copy.start()

    def matrix(rows, columns, rule):
        r = lax.broadcasted_iota(jnp.int32, (2 * rows, columns), 0) % rows
        c = lax.broadcasted_iota(jnp.int32, (2 * rows, columns), 1)
        return jnp.where(rule(r, c), 1.0, 0.0).astype(BF16)

    MR[...] = matrix(256, 128, lambda r, c: r // 2 == c)
    M3[...] = matrix(128, 128, lambda r, c: (r % 2 == 0) & (r // 4 == c % 32))
    MP1[...] = matrix(128, 256, lambda r, c: r == c // 2)
    MP3[...] = matrix(128, 512, lambda r, c: (r // 32 == c // 128) & (r % 32 == (c % 128) // 4))

    def restrict_zero(ref, scale):
        pairs = [
            jnp.concatenate([ref[3 + 2 * k, h, 4:20] + ref[4 + 2 * k, h, 4:20] for h in range(2)], axis=1)
            for k in range(8)
        ]
        TR[0:8, 0:16] = mm(jnp.concatenate(pairs, axis=0), MR[...]).reshape(8, 16, 128)
        return (TR[0:8, pl.ds(0, 8, stride=2), :] + TR[0:8, pl.ds(1, 8, stride=2), :]) * scale

    def restrict_one(ref, x0, count, y0, rows, scale):
        for k in range(count):
            TR[k, 0:rows] = ref[x0 + 2 * k, y0 : y0 + rows] + ref[x0 + 1 + 2 * k, y0 : y0 + rows]
        half = rows // 2
        s = (TR[0:count, pl.ds(0, half, stride=2), :] + TR[0:count, pl.ds(1, half, stride=2), :]) * scale
        return s + jnp.where(lane(s.shape) % 2 == 0, pltpu.roll(s, 127, 2), pltpu.roll(s, 1, 2))

    def restrict_two(ref, scale):
        pairs = jnp.concatenate([ref[4] + ref[5], ref[6] + ref[7]], axis=0)
        s = mm(pairs, M3[...]) * scale
        group = lax.broadcasted_iota(jnp.int32, (1, 128), 1) // 32
        row = jnp.zeros((1, 128), F32)
        for g in range(4):
            at = 16 * (g // 2) + 4 + 2 * (g % 2)
            row = jnp.where(group == g, s[at : at + 1] + s[at + 1 : at + 2], row)
        return row

    def z_copy(ref, k, sems):
        src = ref.at[NZC // 2, yc, pl.ds(gx, 1), :]
        dst = ref.at[(NZC // 2 - k) % NZC, yc, pl.ds(gx, 1), :]
        return remote(src, dst, sems.at[0], sems.at[1], along_z(k))

    def plane_copy(ref, dx, dy, sems):
        part = ref.at[:, yc, pl.ds(gx, 1), :]
        return remote(part, part, sems.at[2], sems.at[3], (columns[dx], rows[dy]))

    def start_z(ref, sems):
        for k in Z_FAR_FIRST:
            z_copy(ref, k, sems).start()

    def start_plane(ref, sems):
        for dx, dy in FAR_FIRST:
            plane_copy(ref, dx, dy, sems).start()

    def all_bytes(kind, sem):
        part = ROWS.at[0, pl.ds(0, NZC - 1), :] if kind == 0 else ROWS
        pltpu.make_async_copy(part, part, sem).wait()

    def landed_z(sems):
        all_bytes(0, sems.at[1])

    def landed_plane(sems):
        all_bytes(1, sems.at[3])

    def sent(sems):
        all_bytes(0, sems.at[0])
        all_bytes(1, sems.at[2])

    C1[8:16, 8:16] = restrict_zero(C0, 0.125 * 0.25)
    c1 = exchange(C1, (8, 8), 8, 8, c1s, c1r)
    C2[4:8, 4:8] = restrict_one(C1, 8, 4, 8, 8, 0.125 * 0.25)
    GC[NZC // 2, yc, pl.ds(gx, 1), :] = restrict_two(C2, 0.125 * 0.25)
    start_z(GC, cg)

    for copy in e0c:
        copy.wait_recv()
    for copy in c1:
        copy.start()
    coefficients(C0, CX0, CY0, CZ0, W0, 22)
    for copy in e0v + e0b:
        copy.wait_recv()
    zero = (B0, CX0, CY0, CZ0)
    sweep(V0, VA0, *zero, W0, 1, 21)
    sweep(VA0, VB0, *zero, W0, 2, 20)
    flux_loop(VB0, *zero, 3, 19, lambda x, v, r: put(VA0, x, r))
    B1[8:16, 8:16] = restrict_zero(VA0, 0.125)
    b1 = exchange(B1, (8, 8), 8, 6, b1s, b1r, 5)
    for copy in b1:
        copy.start()

    h0 = [
        remote(VB0.at[pl.ds(sx, nx), :, pl.ds(sy, ny), :], VH.at[pl.ds(tx, nx), :, pl.ds(ty, ny), :],
               h0s.at[i], h0r.at[i], beside(*o))
        for i, (o, (sx, tx, nx), (sy, ty, ny)) in enumerate((
            ((0, 1), (3, 3, 16), (18, 2, 1)),
            ((0, -1), (3, 3, 16), (5, 21, 1)),
            ((1, 0), (17, 1, 1), (4, 4, 16)),
            ((-1, 0), (4, 20, 1), (4, 4, 16)),
            ((1, 1), (18, 2, 1), (19, 3, 1)),
            ((1, -1), (18, 2, 1), (4, 20, 1)),
            ((-1, 1), (3, 19, 1), (19, 3, 1)),
            ((-1, -1), (3, 19, 1), (4, 20, 1)),
        ))
    ]
    for copy in h0:
        copy.start()

    landed_z(cg)
    start_plane(GC, cg)

    for copy in c1:
        copy.wait_recv()
    coefficients(C1, CX1, CY1, CZ1, W1, 24)
    for k in range(3):
        C2[4 * k : 4 * k + 4, 0:12] = restrict_one(C1, 8 * k, 4, 0, 24, 0.125 * 0.25)
    coefficients(C2, CX2, CY2, CZ2, W2, 12)

    for copy in b1:
        copy.wait_recv()

    def from_zero(to_ref, b_ref, w_ref, lo, hi):
        to_ref[lo:hi] = w_ref[lo:hi] * b_ref[lo:hi]

    one = (B1, CX1, CY1, CZ1)
    from_zero(VA1, B1, W1, 2, 22)
    sweep(VA1, VB1, *one, W1, 3, 21)
    flux_loop(VB1, *one, 4, 20, lambda x, v, r: put(R1, x, r))
    B2[2:10, 0:12] = restrict_one(R1, 4, 8, 0, 24, 0.125)

    two = (B2, CX2, CY2, CZ2)
    from_zero(VA2, B2, W2, 2, 10)
    sweep(VA2, VB2, *two, W2, 3, 9)
    flux_loop(VB2, *two, 4, 8, lambda x, v, r: put(R2, x, r))
    GB[NZC // 2, yc, pl.ds(gx, 1), :] = restrict_two(R2, 0.125)
    start_z(GB, bg)
    B2H[4:8, 4:8] = B2[4:8, 4:8]
    V2H[4:8, 4:8] = VB2[4:8, 4:8]
    h2 = exchange(B2H, (4, 4), 4, 4, h2s.at[0], h2r.at[0]) + exchange(V2H, (4, 4), 4, 4, h2s.at[1], h2r.at[1])
    for copy in h2:
        copy.start()

    landed_plane(cg)
    C3[1 : GY + 1] = GC[...].reshape(GY, GX, 128)
    wrap_rows(C3)
    whole_coefficients(THREE, C3, K3)
    C4[1 : GY + 1] = coarsen_lanes(C3[1 : GY + 1]) * (0.125 * 0.25)
    wrap_rows(C4)
    whole_coefficients(FOUR, C4, K4)

    landed_z(bg)
    start_plane(GB, bg)
    landed_plane(bg)

    b3 = GB[...].reshape(GY, GX, 128)
    mean = jnp.sum(jnp.sum(b3, axis=0), keepdims=True) * (1.0 / (GY * GX * 128))
    B3[1 : GY + 1] = b3
    V3A[1 : GY + 1] = K3[7] * b3
    wrap_rows(V3A)
    whole_sweep(THREE, V3A, V3B, B3, K3, 5, 31)

    def residual(lo, hi, v, s):
        r = B3[lo + 1 : hi + 1] + s - K3[6, lo:hi] * v
        B4[lo + 1 : hi + 1] = coarsen_lanes(r) * 0.125

    whole_sum(THREE, V3B, K3, residual, 6, 30)

    b4 = B4[7:31] - mean
    B4[7:31] = b4
    V4A[7:31] = K4[7, 6:30] * b4
    here, there = V4A, V4B
    for i in range(7):
        whole_sweep(FOUR, here, there, B4, K4, 7 + i, 29 - i)
        here, there = there, here

    V3B[14:24] = V3B[14:24] + here[14:24]
    whole_sweep(THREE, V3B, V3A, B3, K3, 14, 22)
    whole_sweep(THREE, V3A, V3B, B3, K3, 15, 21)

    near = [
        pltpu.roll(V3B[4 * (NZC // 2) + yc + j], lax.rem(1 - gx + GX, GX), 0) for j in range(3)
    ]
    u = mm(jnp.concatenate(near, axis=0), MP3[...])
    for copy in h2:
        copy.wait_recv()
    pair = lax.broadcasted_iota(jnp.int32, (16, 128), 0) // 2
    for x3 in range(6):
        i, dx = x3 // 2, x3 % 2
        rise = jnp.zeros((16, 128), F32)
        for y3 in range(6):
            j, g = y3 // 2, 2 * dx + y3 % 2
            rise = jnp.where(pair == y3, u[8 * j + i : 8 * j + i + 1, 128 * g : 128 * g + 128], rise)
        for x in (2 * x3, 2 * x3 + 1):
            VA2[x] = V2H[x] + rise
    two = (B2H, CX2, CY2, CZ2)
    sweep(VA2, R2, *two, W2, 1, 11)
    sweep(R2, VA2, *two, W2, 2, 10)

    for k in range(8):
        cells = VA2[2 + k, 0:12, :]
        TP1[k, pl.ds(0, 12, stride=2), :] = cells
        TP1[k, pl.ds(1, 12, stride=2), :] = cells
    for x in range(5, 19):
        VA1[x] = VB1[x] + TP1[x // 2 - 2]
    sweep(VA1, R1, *one, W1, 6, 18)
    sweep(R1, VA1, *one, W1, 7, 17)

    for k in range(10):
        cells = VA1[7 + k, 7:17, :]
        TP0[k, pl.ds(2, 10, stride=2), :] = cells
        TP0[k, pl.ds(3, 10, stride=2), :] = cells
    u = mm(TP0[...].reshape(10 * 24, 128), MP1[...])
    for h in range(2):
        PE0[:, h] = u[:, 128 * h : 128 * h + 128].reshape(10, 24, 128)
    for copy in h0:
        copy.wait_recv()
    row = lax.broadcasted_iota(jnp.int32, (24, 128), 0)
    outer = (row == 2) | (row == 21)

    def raise_slab(x, carry):
        for h in range(2):
            VA0[x, h] = jnp.where(outer, VH[x, h], VB0[x, h]) + PE0[lax.div(x - 1, 2), h]
        return carry

    lax.fori_loop(3, 19, raise_slab, 0, unroll=8)
    corner = (row == 3) | (row == 20)
    for h in range(2):
        for x in (1, 20):
            VA0[x, h] = VH[x, h] + PE0[(x - 1) // 2, h]
        for x in (2, 19):
            VA0[x, h] = jnp.where(corner, VH[x, h], VB0[x, h]) + PE0[(x - 1) // 2, h]
    for copy in e0c + e0v + e0b:
        copy.wait_send()
    sweep(VA0, V0, *zero, W0, 2, 20)

    def last(x, v, r):
        s = add(v, mul(get(W0, x), r))
        for h in range(2):
            out_ref[x - 3, :, 128 * h : 128 * h + 128] = s[h][4:20]

    flux_loop(V0, *zero, 3, 19, last)

    for copy in c1 + b1 + h0 + h2:
        copy.wait_send()
    sent(cg)
    sent(bg)


def solution(mesh):
    def vmem(*shape):
        return pltpu.VMEM(shape, F32)

    def half(*shape):
        return pltpu.VMEM(shape, BF16)

    dma = pltpu.SemaphoreType.DMA
    scratch = (
        [vmem(22, 2, 24, 128)] * 10
        + [vmem(8, 24, 128), vmem(10, 2, 24, 128), vmem(10, 24, 128)]
        + [vmem(24, 24, 128)] * 9
        + [vmem(8, 24, 128)]
        + [vmem(12, 16, 128)] * 11
        + [vmem(GY + 2, GX, 128)] * 4
        + [vmem(8, GY, GX, 128)]
        + [vmem(GY + 2, GX, 128)] * 4
        + [vmem(8, GY, GX, 128)]
        + [vmem(NZC, NYC, GX, 128)] * 2
        + [half(512, 128), half(256, 128), half(256, 256), half(256, 512)]
        + [vmem(GX * NYC - 1, NZC, 128)]
        + [dma((6,)), dma((3, 8)), dma((3, 8))]
        + [dma((8,))] * 6
        + [dma((2, 8))] * 2
        + [dma((4,))] * 2
    )

    def step(source, conductivity, guess):
        return pl.pallas_call(
            kernel,
            out_shape=jax.ShapeDtypeStruct(source.shape, F32),
            in_specs=[pl.BlockSpec(memory_space=pl.ANY)] * 3,
            out_specs=pl.BlockSpec(memory_space=pltpu.VMEM),
            scratch_shapes=scratch,
            compiler_params=pltpu.CompilerParams(
                collective_id=0, has_side_effects=True, vmem_limit_bytes=54848 * 2**10
            ),
            name="vcycle",
        )(source, conductivity, guess)

    spec = P("gx", "gy", None)
    return jax.shard_map(step, mesh=mesh, in_specs=(spec, spec, spec), out_specs=spec, check_vma=False)
```

```python
import jax
import jax.numpy as jnp
from jax import lax
from jax.experimental import pallas as pl
from jax.experimental.pallas import tpu as pltpu
from jax.sharding import PartitionSpec as P

MESH = pl.DeviceIdType.MESH
F32, BF16 = jnp.float32, jnp.bfloat16
OMEGA = 0.8
GX, GY, NYC, NZC = 8, 32, 4, 8
FAR_FIRST = sorted(
    ((dx, dy) for dx in range(GX) for dy in range(NYC) if dx or dy),
    key=lambda o: -(min(o[0], GX - o[0]) + 2 * min(o[1], NYC - o[1])),
)
EIGHT = [(1, 1), (1, -1), (-1, 1), (-1, -1), (0, 1), (0, -1), (1, 0), (-1, 0)]
Z_FAR_FIRST = (4, 3, 5, 2, 6, 1, 7)


def harmonic(a, b):
    return 2.0 * a * b / (a + b)


def mm(a, m):
    hi = a.astype(BF16)
    lo = (a - hi.astype(F32)).astype(BF16)
    return jnp.dot(jnp.concatenate([hi, lo], axis=1), m, preferred_element_type=F32)


def zp(s):
    if len(s) == 1:
        return (pltpu.roll(s[0], 126 if s[0].shape[0] == 16 else 127, 1),)
    last = lax.broadcasted_iota(jnp.int32, s[0].shape, 1) == 127
    a, b = pltpu.roll(s[0], 127, 1), pltpu.roll(s[1], 127, 1)
    return (jnp.where(last, b, a), jnp.where(last, a, b))


def zm(s):
    if len(s) == 1:
        return (pltpu.roll(s[0], 2 if s[0].shape[0] == 16 else 1, 1),)
    first = lax.broadcasted_iota(jnp.int32, s[0].shape, 1) == 0
    a, b = pltpu.roll(s[0], 1, 1), pltpu.roll(s[1], 1, 1)
    return (jnp.where(first, b, a), jnp.where(first, a, b))


def yp(s):
    return tuple(pltpu.roll(a, a.shape[0] - 1, 0) for a in s)


def ym(s):
    return tuple(pltpu.roll(a, 1, 0) for a in s)


def each(f, *slabs):
    return tuple(f(*a) for a in zip(*slabs))


def get(ref, x):
    if len(ref.shape) == 4:
        return (ref[x, 0], ref[x, 1])
    return (ref[x],)


def put(ref, x, s):
    if len(ref.shape) == 4:
        ref[x, 0] = s[0]
        ref[x, 1] = s[1]
    else:
        ref[x] = s[0]


def add(a, b):
    return each(lambda p, q: p + q, a, b)


def sub(a, b):
    return each(lambda p, q: p - q, a, b)


def mul(a, b):
    return each(lambda p, q: p * q, a, b)


def steps_of(count, most):
    return max(n for n in range(1, most + 1) if count % n == 0)


def coefficients(c_ref, cx_ref, cy_ref, cz_ref, w_ref, slabs):
    c = get(c_ref, 0)
    n = get(c_ref, 1)
    first = each(harmonic, c, n)
    put(cx_ref, 0, first)

    def body(x, carry):
        c, before = carry
        n = get(c_ref, x + 1)
        ex = each(harmonic, c, n)
        ey = each(harmonic, c, yp(c))
        ez = each(harmonic, c, zp(c))
        d = add(add(add(ex, before), add(ey, ym(ey))), add(ez, zm(ez)))
        put(cx_ref, x, ex)
        put(cy_ref, x, ey)
        put(cz_ref, x, ez)
        put(w_ref, x, each(lambda p: OMEGA / p, d))
        return n, ex

    lax.fori_loop(1, slabs - 1, body, (n, first), unroll=steps_of(slabs - 2, UNROLL_FACES[len(c_ref.shape)]))


def flux_loop(v_ref, b_ref, cx_ref, cy_ref, cz_ref, lo, hi, emit):
    v = get(v_ref, lo)
    before = mul(get(cx_ref, lo - 1), sub(v, get(v_ref, lo - 1)))

    def body(x, carry):
        v, before = carry
        n = get(v_ref, x + 1)
        tx = mul(get(cx_ref, x), sub(n, v))
        ty = mul(get(cy_ref, x), sub(yp(v), v))
        tz = mul(get(cz_ref, x), sub(zp(v), v))
        r = add(add(sub(tx, before), sub(ty, ym(ty))), sub(tz, zm(tz)))
        emit(x, v, add(get(b_ref, x), r))
        return n, tx

    lax.fori_loop(lo, hi, body, (v, before), unroll=steps_of(hi - lo, UNROLL[len(v_ref.shape)]))


def sweep(v_ref, to_ref, b_ref, cx_ref, cy_ref, cz_ref, w_ref, lo, hi):
    def emit(x, v, r):
        put(to_ref, x, add(v, mul(get(w_ref, x), r)))

    flux_loop(v_ref, b_ref, cx_ref, cy_ref, cz_ref, lo, hi, emit)


def lane(shape):
    return lax.broadcasted_iota(jnp.int32, shape, len(shape) - 1)


def three_zp(v):
    return jnp.where(lane(v.shape) % 32 == 31, pltpu.roll(v, 31, 2), pltpu.roll(v, 127, 2))


def three_zm(v):
    return jnp.where(lane(v.shape) % 32 == 0, pltpu.roll(v, 97, 2), pltpu.roll(v, 1, 2))


def three_xp(v):
    r = pltpu.roll(v, 64, 2)
    return jnp.where(lane(v.shape) < 64, r, pltpu.roll(r, GX - 1, 1))


def three_xm(v):
    r = pltpu.roll(v, 64, 2)
    return jnp.where(lane(v.shape) < 64, pltpu.roll(r, 1, 1), r)


def three_y(v):
    up, down = pltpu.roll(v, 96, 2), pltpu.roll(v, 32, 2)
    first = lane(v[1:-1].shape) % 64 < 32
    return (jnp.where(first, up[1:-1], down[2:]), jnp.where(first, up[:-2], down[1:-1]))


def four_zp(v):
    return pltpu.roll(v, 126, 2)


def four_zm(v):
    return pltpu.roll(v, 2, 2)


def four_xp(v):
    return pltpu.roll(v, GX - 1, 1)


def four_xm(v):
    return pltpu.roll(v, 1, 1)


def four_y(v):
    return v[2:], v[:-2]


THREE = (three_xp, three_xm, three_y, three_zp, three_zm)
FOUR = (four_xp, four_xm, four_y, four_zp, four_zm)
UNROLL = {4: 10, 3: 20}
UNROLL_FACES = {4: 10, 3: 11}


def wrap_rows(ref):
    ref[0] = ref[GY]
    ref[GY + 1] = ref[1]


def chunks(lo, hi):
    parts = -(-(hi - lo) // 16)
    cuts = [lo + (hi - lo) * i // parts for i in range(parts + 1)]
    return list(zip(cuts[:-1], cuts[1:]))


def whole_coefficients(level, c_ref, k_ref):
    xp, xm, y, zplus, zminus = level
    for lo, hi in chunks(0, GY):
        ext = c_ref[lo : hi + 2]
        c = ext[1:-1]
        up, down = y(ext)
        ex = harmonic(c, xp(c))
        ez = harmonic(c, zplus(c))
        ey, wy = harmonic(c, up), harmonic(down, c)
        wx, wz = xm(ex), zminus(ez)
        d = (ex + wx) + (ey + wy) + (ez + wz)
        for j, value in enumerate((ex, wx, ey, wy, ez, wz, d, OMEGA / d)):
            k_ref[j, lo:hi] = value


def whole_sum(level, v_ref, k_ref, emit, first, last):
    xp, xm, y, zplus, zminus = level
    for lo, hi in chunks(first, last):
        ext = v_ref[lo : hi + 2]
        v = ext[1:-1]
        up, down = y(ext)
        k = [k_ref[j, lo:hi] for j in range(6)]
        s = (k[0] * xp(v) + k[1] * xm(v)) + (k[2] * up + k[3] * down)
        emit(lo, hi, v, s + (k[4] * zplus(v) + k[5] * zminus(v)))


def whole_sweep(level, v_ref, to_ref, b_ref, k_ref, first=0, last=GY):
    def emit(lo, hi, v, s):
        to_ref[lo + 1 : hi + 1] = (1.0 - OMEGA) * v + k_ref[7, lo:hi] * (b_ref[lo + 1 : hi + 1] + s)

    whole_sum(level, v_ref, k_ref, emit, first, last)
    if last - first == GY:
        wrap_rows(to_ref)


def coarsen_lanes(v):
    s = v + pltpu.roll(v, 64, 2)
    s = s + pltpu.roll(s, 32, 2)
    return s + jnp.where(lane(v.shape) % 2 == 0, pltpu.roll(s, 127, 2), pltpu.roll(s, 1, 2))


def kernel(
    src_ref, cond_ref, guess_ref, out_ref,
    V0, B0, C0, CX0, CY0, CZ0, W0, VA0, VB0, VH, TR, PE0, TP0,
    C1, CX1, CY1, CZ1, W1, B1, VA1, VB1, R1, TP1,
    C2, CX2, CY2, CZ2, W2, B2, VA2, VB2, R2, B2H, V2H,
    C3, B3, V3A, V3B, K3, C4, B4, V4A, V4B, K4, GC, GB,
    MR, M3, MP1, MP3, ROWS,
    lsem, e0s, e0r, c1s, c1r, b1s, b1r, h0s, h0r, h2s, h2r, cg, bg,
):
    gx, gy = lax.axis_index("gx"), lax.axis_index("gy")
    yc, zc = lax.rem(gy, NYC), lax.div(gy, NYC)

    def beside(dx, dy):
        return (lax.rem(gx + dx + GX, GX), lax.rem(gy + dy + GY, GY))

    def along_z(k):
        return (gx, lax.rem(zc + k, NZC) * NYC + yc)

    def remote(src, dst, send, recv, device):
        return pltpu.make_async_remote_copy(
            src_ref=src, dst_ref=dst, send_sem=send, recv_sem=recv, device_id=device, device_id_type=MESH
        )

    loads = []
    for i, (ref, to) in enumerate(((cond_ref, C0), (guess_ref, V0), (src_ref, B0))):
        for h in range(2):
            loads.append(
                pltpu.make_async_copy(
                    ref.at[:, :, pl.ds(128 * h, 128)],
                    to.at[pl.ds(3, 16), h, pl.ds(4, 16), :],
                    lsem.at[2 * i + h],
                )
            )
    barrier = pltpu.get_barrier_semaphore()
    for dx, dy in EIGHT:
        pl.semaphore_signal(barrier, inc=1, device_id=beside(dx, dy), device_id_type=MESH)

    columns = [lax.rem(gx + d, GX) for d in range(GX)]
    rows = [zc * NYC + lax.rem(yc + d, NYC) for d in range(NYC)]
    for dx, dy in FAR_FIRST:
        pl.semaphore_signal(barrier, inc=1, device_id=(columns[dx], rows[dy]), device_id_type=MESH)
    for k in Z_FAR_FIRST:
        pl.semaphore_signal(barrier, inc=1, device_id=along_z(k), device_id_type=MESH)
    for copy in loads:
        copy.start()

    pl.semaphore_wait(barrier, len(EIGHT) + GX * NYC - 1 + NZC - 1)

    def edge(base, extent, step, width):
        if step == 0:
            return base, base, extent
        if step == 1:
            return base + extent - width, base - width, width
        return base, base + extent, width

    def block_copy(ref, base, extent, step, width, send, recv):
        sx, tx, nx = edge(base[0], extent, step[0], width)
        sy, ty, ny = edge(base[1], extent, step[1], width)
        if len(ref.shape) == 4:
            src, dst = ref.at[pl.ds(sx, nx), :, pl.ds(sy, ny), :], ref.at[pl.ds(tx, nx), :, pl.ds(ty, ny), :]
        else:
            src, dst = ref.at[pl.ds(sx, nx), pl.ds(sy, ny), :], ref.at[pl.ds(tx, nx), pl.ds(ty, ny), :]
        return remote(src, dst, send, recv, beside(*step))

    def exchange(ref, base, extent, width, send, recv, corner=None):
        return [
            block_copy(ref, base, extent, o, corner if corner and o[0] and o[1] else width, send.at[i], recv.at[i])
            for i, o in enumerate(EIGHT)
        ]

    e0c = exchange(C0, (3, 4), 16, 3, e0s.at[0], e0r.at[0], 2)
    e0v = exchange(V0, (3, 4), 16, 3, e0s.at[1], e0r.at[1], 2)
    e0b = exchange(B0, (3, 4), 16, 2, e0s.at[2], e0r.at[2], 1)
    for first in (0, 4, 6):
        for n, copies in enumerate((e0c, e0v, e0b)):
            if first == 0:
                loads[2 * n].wait()
                loads[2 * n + 1].wait()
            for copy in copies[first : first + 4 if first == 0 else first + 2]:
                copy.start()

    def matrix(rows, columns, rule):
        r = lax.broadcasted_iota(jnp.int32, (2 * rows, columns), 0) % rows
        c = lax.broadcasted_iota(jnp.int32, (2 * rows, columns), 1)
        return jnp.where(rule(r, c), 1.0, 0.0).astype(BF16)

    MR[...] = matrix(256, 128, lambda r, c: r // 2 == c)
    M3[...] = matrix(128, 128, lambda r, c: (r % 2 == 0) & (r // 4 == c % 32))
    MP1[...] = matrix(128, 256, lambda r, c: r == c // 2)
    MP3[...] = matrix(128, 512, lambda r, c: (r // 32 == c // 128) & (r % 32 == (c % 128) // 4))

    def restrict_zero(ref, scale):
        pairs = [
            jnp.concatenate([ref[3 + 2 * k, h, 4:20] + ref[4 + 2 * k, h, 4:20] for h in range(2)], axis=1)
            for k in range(8)
        ]
        TR[0:8, 0:16] = mm(jnp.concatenate(pairs, axis=0), MR[...]).reshape(8, 16, 128)
        return (TR[0:8, pl.ds(0, 8, stride=2), :] + TR[0:8, pl.ds(1, 8, stride=2), :]) * scale

    def restrict_one(ref, x0, count, y0, rows, scale):
        for k in range(count):
            TR[k, 0:rows] = ref[x0 + 2 * k, y0 : y0 + rows] + ref[x0 + 1 + 2 * k, y0 : y0 + rows]
        half = rows // 2
        s = (TR[0:count, pl.ds(0, half, stride=2), :] + TR[0:count, pl.ds(1, half, stride=2), :]) * scale
        return s + jnp.where(lane(s.shape) % 2 == 0, pltpu.roll(s, 127, 2), pltpu.roll(s, 1, 2))

    def restrict_two(ref, scale):
        pairs = jnp.concatenate([ref[4] + ref[5], ref[6] + ref[7]], axis=0)
        s = mm(pairs, M3[...]) * scale
        group = lax.broadcasted_iota(jnp.int32, (1, 128), 1) // 32
        row = jnp.zeros((1, 128), F32)
        for g in range(4):
            at = 16 * (g // 2) + 4 + 2 * (g % 2)
            row = jnp.where(group == g, s[at : at + 1] + s[at + 1 : at + 2], row)
        return row

    def z_copy(ref, k, sems):
        src = ref.at[NZC // 2, yc, pl.ds(gx, 1), :]
        dst = ref.at[(NZC // 2 - k) % NZC, yc, pl.ds(gx, 1), :]
        return remote(src, dst, sems.at[0], sems.at[1], along_z(k))

    def plane_copy(ref, dx, dy, sems):
        part = ref.at[:, yc, pl.ds(gx, 1), :]
        return remote(part, part, sems.at[2], sems.at[3], (columns[dx], rows[dy]))

    def start_z(ref, sems):
        for k in Z_FAR_FIRST:
            z_copy(ref, k, sems).start()

    def start_plane(ref, sems):
        for dx, dy in FAR_FIRST:
            plane_copy(ref, dx, dy, sems).start()

    def all_bytes(kind, sem):
        part = ROWS.at[0, pl.ds(0, NZC - 1), :] if kind == 0 else ROWS
        pltpu.make_async_copy(part, part, sem).wait()

    def landed_z(sems):
        all_bytes(0, sems.at[1])

    def landed_plane(sems):
        all_bytes(1, sems.at[3])

    def sent(sems):
        all_bytes(0, sems.at[0])
        all_bytes(1, sems.at[2])

    C1[8:16, 8:16] = restrict_zero(C0, 0.125 * 0.25)
    c1 = exchange(C1, (8, 8), 8, 8, c1s, c1r)
    C2[4:8, 4:8] = restrict_one(C1, 8, 4, 8, 8, 0.125 * 0.25)
    GC[NZC // 2, yc, pl.ds(gx, 1), :] = restrict_two(C2, 0.125 * 0.25)
    start_z(GC, cg)

    for copy in e0c:
        copy.wait_recv()
    for copy in c1:
        copy.start()
    coefficients(C0, CX0, CY0, CZ0, W0, 22)
    for copy in e0v + e0b:
        copy.wait_recv()
    zero = (B0, CX0, CY0, CZ0)
    sweep(V0, VA0, *zero, W0, 1, 21)
    sweep(VA0, VB0, *zero, W0, 2, 20)
    flux_loop(VB0, *zero, 3, 19, lambda x, v, r: put(VA0, x, r))
    B1[8:16, 8:16] = restrict_zero(VA0, 0.125)
    b1 = exchange(B1, (8, 8), 8, 6, b1s, b1r, 5)
    for copy in b1:
        copy.start()

    h0 = [
        remote(VB0.at[pl.ds(sx, nx), :, pl.ds(sy, ny), :], VH.at[pl.ds(tx, nx), :, pl.ds(ty, ny), :],
               h0s.at[i], h0r.at[i], beside(*o))
        for i, (o, (sx, tx, nx), (sy, ty, ny)) in enumerate((
            ((0, 1), (3, 3, 16), (18, 2, 1)),
            ((0, -1), (3, 3, 16), (5, 21, 1)),
            ((1, 0), (17, 1, 1), (4, 4, 16)),
            ((-1, 0), (4, 20, 1), (4, 4, 16)),
            ((1, 1), (18, 2, 1), (19, 3, 1)),
            ((1, -1), (18, 2, 1), (4, 20, 1)),
            ((-1, 1), (3, 19, 1), (19, 3, 1)),
            ((-1, -1), (3, 19, 1), (4, 20, 1)),
        ))
    ]

    landed_z(cg)
    start_plane(GC, cg)

    for copy in c1:
        copy.wait_recv()
    coefficients(C1, CX1, CY1, CZ1, W1, 24)
    for k in range(3):
        C2[4 * k : 4 * k + 4, 0:12] = restrict_one(C1, 8 * k, 4, 0, 24, 0.125 * 0.25)
    coefficients(C2, CX2, CY2, CZ2, W2, 12)

    for copy in b1:
        copy.wait_recv()

    def from_zero(to_ref, b_ref, w_ref, lo, hi):
        to_ref[lo:hi] = w_ref[lo:hi] * b_ref[lo:hi]

    one = (B1, CX1, CY1, CZ1)
    from_zero(VA1, B1, W1, 2, 22)
    sweep(VA1, VB1, *one, W1, 3, 21)
    flux_loop(VB1, *one, 4, 20, lambda x, v, r: put(R1, x, r))
    B2[2:10, 0:12] = restrict_one(R1, 4, 8, 0, 24, 0.125)

    two = (B2, CX2, CY2, CZ2)
    from_zero(VA2, B2, W2, 2, 10)
    sweep(VA2, VB2, *two, W2, 3, 9)
    flux_loop(VB2, *two, 4, 8, lambda x, v, r: put(R2, x, r))
    GB[NZC // 2, yc, pl.ds(gx, 1), :] = restrict_two(R2, 0.125)
    start_z(GB, bg)
    for copy in h0:
        copy.start()
    B2H[4:8, 4:8] = B2[4:8, 4:8]
    V2H[4:8, 4:8] = VB2[4:8, 4:8]
    h2 = exchange(B2H, (4, 4), 4, 4, h2s.at[0], h2r.at[0]) + exchange(V2H, (4, 4), 4, 4, h2s.at[1], h2r.at[1])
    for copy in h2:
        copy.start()

    landed_plane(cg)
    C3[1 : GY + 1] = GC[...].reshape(GY, GX, 128)
    wrap_rows(C3)
    whole_coefficients(THREE, C3, K3)
    C4[1 : GY + 1] = coarsen_lanes(C3[1 : GY + 1]) * (0.125 * 0.25)
    wrap_rows(C4)
    whole_coefficients(FOUR, C4, K4)

    landed_z(bg)
    start_plane(GB, bg)
    landed_plane(bg)

    b3 = GB[...].reshape(GY, GX, 128)
    mean = jnp.sum(jnp.sum(b3, axis=0), keepdims=True) * (1.0 / (GY * GX * 128))
    B3[1 : GY + 1] = b3
    V3A[1 : GY + 1] = K3[7] * b3
    wrap_rows(V3A)
    whole_sweep(THREE, V3A, V3B, B3, K3, 5, 31)

    def residual(lo, hi, v, s):
        r = B3[lo + 1 : hi + 1] + s - K3[6, lo:hi] * v
        B4[lo + 1 : hi + 1] = coarsen_lanes(r) * 0.125

    whole_sum(THREE, V3B, K3, residual, 6, 30)

    b4 = B4[7:31] - mean
    B4[7:31] = b4
    V4A[7:31] = K4[7, 6:30] * b4
    here, there = V4A, V4B
    for i in range(7):
        whole_sweep(FOUR, here, there, B4, K4, 7 + i, 29 - i)
        here, there = there, here

    V3B[14:24] = V3B[14:24] + here[14:24]
    whole_sweep(THREE, V3B, V3A, B3, K3, 14, 22)
    whole_sweep(THREE, V3A, V3B, B3, K3, 15, 21)

    near = [
        pltpu.roll(V3B[4 * (NZC // 2) + yc + j], lax.rem(1 - gx + GX, GX), 0) for j in range(3)
    ]
    u = mm(jnp.concatenate(near, axis=0), MP3[...])
    for copy in h2:
        copy.wait_recv()
    pair = lax.broadcasted_iota(jnp.int32, (16, 128), 0) // 2
    for x3 in range(6):
        i, dx = x3 // 2, x3 % 2
        rise = jnp.zeros((16, 128), F32)
        for y3 in range(6):
            j, g = y3 // 2, 2 * dx + y3 % 2
            rise = jnp.where(pair == y3, u[8 * j + i : 8 * j + i + 1, 128 * g : 128 * g + 128], rise)
        for x in (2 * x3, 2 * x3 + 1):
            VA2[x] = V2H[x] + rise
    two = (B2H, CX2, CY2, CZ2)
    sweep(VA2, R2, *two, W2, 1, 11)
    sweep(R2, VA2, *two, W2, 2, 10)

    for k in range(8):
        cells = VA2[2 + k, 0:12, :]
        TP1[k, pl.ds(0, 12, stride=2), :] = cells
        TP1[k, pl.ds(1, 12, stride=2), :] = cells
    for x in range(5, 19):
        VA1[x] = VB1[x] + TP1[x // 2 - 2]
    sweep(VA1, R1, *one, W1, 6, 18)
    sweep(R1, VA1, *one, W1, 7, 17)

    for k in range(10):
        cells = VA1[7 + k, 7:17, :]
        TP0[k, pl.ds(2, 10, stride=2), :] = cells
        TP0[k, pl.ds(3, 10, stride=2), :] = cells
    u = mm(TP0[...].reshape(10 * 24, 128), MP1[...])
    for h in range(2):
        PE0[:, h] = u[:, 128 * h : 128 * h + 128].reshape(10, 24, 128)
    for copy in h0:
        copy.wait_recv()
    row = lax.broadcasted_iota(jnp.int32, (24, 128), 0)
    outer = (row == 2) | (row == 21)

    def raise_slab(x, carry):
        for h in range(2):
            VA0[x, h] = jnp.where(outer, VH[x, h], VB0[x, h]) + PE0[lax.div(x - 1, 2), h]
        return carry

    lax.fori_loop(3, 19, raise_slab, 0, unroll=8)
    corner = (row == 3) | (row == 20)
    for h in range(2):
        for x in (1, 20):
            VA0[x, h] = VH[x, h] + PE0[(x - 1) // 2, h]
        for x in (2, 19):
            VA0[x, h] = jnp.where(corner, VH[x, h], VB0[x, h]) + PE0[(x - 1) // 2, h]
    for copy in e0c + e0v + e0b:
        copy.wait_send()
    sweep(VA0, V0, *zero, W0, 2, 20)

    def last(x, v, r):
        s = add(v, mul(get(W0, x), r))
        for h in range(2):
            out_ref[x - 3, :, 128 * h : 128 * h + 128] = s[h][4:20]

    flux_loop(V0, *zero, 3, 19, last)

    for copy in c1 + b1 + h0 + h2:
        copy.wait_send()
    sent(cg)
    sent(bg)


def solution(mesh):
    def vmem(*shape):
        return pltpu.VMEM(shape, F32)

    def half(*shape):
        return pltpu.VMEM(shape, BF16)

    dma = pltpu.SemaphoreType.DMA
    scratch = (
        [vmem(22, 2, 24, 128)] * 10
        + [vmem(8, 24, 128), vmem(10, 2, 24, 128), vmem(10, 24, 128)]
        + [vmem(24, 24, 128)] * 9
        + [vmem(8, 24, 128)]
        + [vmem(12, 16, 128)] * 11
        + [vmem(GY + 2, GX, 128)] * 4
        + [vmem(8, GY, GX, 128)]
        + [vmem(GY + 2, GX, 128)] * 4
        + [vmem(8, GY, GX, 128)]
        + [vmem(NZC, NYC, GX, 128)] * 2
        + [half(512, 128), half(256, 128), half(256, 256), half(256, 512)]
        + [vmem(GX * NYC - 1, NZC, 128)]
        + [dma((6,)), dma((3, 8)), dma((3, 8))]
        + [dma((8,))] * 6
        + [dma((2, 8))] * 2
        + [dma((4,))] * 2
    )

    def step(source, conductivity, guess):
        return pl.pallas_call(
            kernel,
            out_shape=jax.ShapeDtypeStruct(source.shape, F32),
            in_specs=[pl.BlockSpec(memory_space=pl.ANY)] * 3,
            out_specs=pl.BlockSpec(memory_space=pltpu.VMEM),
            scratch_shapes=scratch,
            compiler_params=pltpu.CompilerParams(
                collective_id=0, has_side_effects=True, vmem_limit_bytes=54848 * 2**10
            ),
            name="vcycle",
        )(source, conductivity, guess)

    spec = P("gx", "gy", None)
    return jax.shard_map(step, mesh=mesh, in_specs=(spec, spec, spec), out_specs=spec, check_vma=False)
```

```python
import jax
import jax.numpy as jnp
from jax import lax
from jax.experimental import pallas as pl
from jax.experimental.pallas import tpu as pltpu
from jax.sharding import PartitionSpec as P

MESH = pl.DeviceIdType.MESH
F32, BF16 = jnp.float32, jnp.bfloat16
OMEGA = 0.8
GX, GY, NYC, NZC = 8, 32, 4, 8
FAR_FIRST = sorted(
    ((dx, dy) for dx in range(GX) for dy in range(NYC) if dx or dy),
    key=lambda o: -(min(o[0], GX - o[0]) + 2 * min(o[1], NYC - o[1])),
)
EIGHT = [(1, 1), (1, -1), (-1, 1), (-1, -1), (0, 1), (0, -1), (1, 0), (-1, 0)]
Z_FAR_FIRST = (4, 3, 5, 2, 6, 1, 7)


def harmonic(a, b):
    return 2.0 * a * b / (a + b)


def mm(a, m):
    hi = a.astype(BF16)
    lo = (a - hi.astype(F32)).astype(BF16)
    return jnp.dot(jnp.concatenate([hi, lo], axis=1), m, preferred_element_type=F32)


def zp(s):
    if len(s) == 1:
        return (pltpu.roll(s[0], 126 if s[0].shape[0] == 16 else 127, 1),)
    last = lax.broadcasted_iota(jnp.int32, s[0].shape, 1) == 127
    a, b = pltpu.roll(s[0], 127, 1), pltpu.roll(s[1], 127, 1)
    return (jnp.where(last, b, a), jnp.where(last, a, b))


def zm(s):
    if len(s) == 1:
        return (pltpu.roll(s[0], 2 if s[0].shape[0] == 16 else 1, 1),)
    first = lax.broadcasted_iota(jnp.int32, s[0].shape, 1) == 0
    a, b = pltpu.roll(s[0], 1, 1), pltpu.roll(s[1], 1, 1)
    return (jnp.where(first, b, a), jnp.where(first, a, b))


def yp(s):
    return tuple(pltpu.roll(a, a.shape[0] - 1, 0) for a in s)


def ym(s):
    return tuple(pltpu.roll(a, 1, 0) for a in s)


def each(f, *slabs):
    return tuple(f(*a) for a in zip(*slabs))


def get(ref, x):
    if len(ref.shape) == 4:
        return (ref[x, 0], ref[x, 1])
    return (ref[x],)


def put(ref, x, s):
    if len(ref.shape) == 4:
        ref[x, 0] = s[0]
        ref[x, 1] = s[1]
    else:
        ref[x] = s[0]


def add(a, b):
    return each(lambda p, q: p + q, a, b)


def sub(a, b):
    return each(lambda p, q: p - q, a, b)


def mul(a, b):
    return each(lambda p, q: p * q, a, b)


def steps_of(count, most):
    return max(n for n in range(1, most + 1) if count % n == 0)


def coefficients(c_ref, cx_ref, cy_ref, cz_ref, w_ref, slabs):
    c = get(c_ref, 0)
    n = get(c_ref, 1)
    first = each(harmonic, c, n)
    put(cx_ref, 0, first)

    def body(x, carry):
        c, before = carry
        n = get(c_ref, x + 1)
        ex = each(harmonic, c, n)
        ey = each(harmonic, c, yp(c))
        ez = each(harmonic, c, zp(c))
        d = add(add(add(ex, before), add(ey, ym(ey))), add(ez, zm(ez)))
        put(cx_ref, x, ex)
        put(cy_ref, x, ey)
        put(cz_ref, x, ez)
        put(w_ref, x, each(lambda p: OMEGA / p, d))
        return n, ex

    lax.fori_loop(1, slabs - 1, body, (n, first), unroll=steps_of(slabs - 2, UNROLL_FACES[len(c_ref.shape)]))


def flux_loop(v_ref, b_ref, cx_ref, cy_ref, cz_ref, lo, hi, emit):
    v = get(v_ref, lo)
    before = mul(get(cx_ref, lo - 1), sub(v, get(v_ref, lo - 1)))

    def body(x, carry):
        v, before = carry
        n = get(v_ref, x + 1)
        tx = mul(get(cx_ref, x), sub(n, v))
        ty = mul(get(cy_ref, x), sub(yp(v), v))
        tz = mul(get(cz_ref, x), sub(zp(v), v))
        r = add(add(sub(tx, before), sub(ty, ym(ty))), sub(tz, zm(tz)))
        emit(x, v, add(get(b_ref, x), r))
        return n, tx

    lax.fori_loop(lo, hi, body, (v, before), unroll=steps_of(hi - lo, UNROLL[len(v_ref.shape)]))


def sweep(v_ref, to_ref, b_ref, cx_ref, cy_ref, cz_ref, w_ref, lo, hi):
    def emit(x, v, r):
        put(to_ref, x, add(v, mul(get(w_ref, x), r)))

    flux_loop(v_ref, b_ref, cx_ref, cy_ref, cz_ref, lo, hi, emit)


def lane(shape):
    return lax.broadcasted_iota(jnp.int32, shape, len(shape) - 1)


def three_zp(v):
    return jnp.where(lane(v.shape) % 32 == 31, pltpu.roll(v, 31, 2), pltpu.roll(v, 127, 2))


def three_zm(v):
    return jnp.where(lane(v.shape) % 32 == 0, pltpu.roll(v, 97, 2), pltpu.roll(v, 1, 2))


def three_xp(v):
    r = pltpu.roll(v, 64, 2)
    return jnp.where(lane(v.shape) < 64, r, pltpu.roll(r, GX - 1, 1))


def three_xm(v):
    r = pltpu.roll(v, 64, 2)
    return jnp.where(lane(v.shape) < 64, pltpu.roll(r, 1, 1), r)


def three_y(v):
    up, down = pltpu.roll(v, 96, 2), pltpu.roll(v, 32, 2)
    first = lane(v[1:-1].shape) % 64 < 32
    return (jnp.where(first, up[1:-1], down[2:]), jnp.where(first, up[:-2], down[1:-1]))


def four_zp(v):
    return pltpu.roll(v, 126, 2)


def four_zm(v):
    return pltpu.roll(v, 2, 2)


def four_xp(v):
    return pltpu.roll(v, GX - 1, 1)


def four_xm(v):
    return pltpu.roll(v, 1, 1)


def four_y(v):
    return v[2:], v[:-2]


THREE = (three_xp, three_xm, three_y, three_zp, three_zm)
FOUR = (four_xp, four_xm, four_y, four_zp, four_zm)
UNROLL = {4: 10, 3: 20}
UNROLL_FACES = {4: 10, 3: 11}


def wrap_rows(ref):
    ref[0] = ref[GY]
    ref[GY + 1] = ref[1]


def chunks(lo, hi):
    parts = -(-(hi - lo) // 16)
    cuts = [lo + (hi - lo) * i // parts for i in range(parts + 1)]
    return list(zip(cuts[:-1], cuts[1:]))


def whole_coefficients(level, c_ref, k_ref):
    xp, xm, y, zplus, zminus = level
    for lo, hi in chunks(0, GY):
        ext = c_ref[lo : hi + 2]
        c = ext[1:-1]
        up, down = y(ext)
        ex = harmonic(c, xp(c))
        ez = harmonic(c, zplus(c))
        ey, wy = harmonic(c, up), harmonic(down, c)
        wx, wz = xm(ex), zminus(ez)
        d = (ex + wx) + (ey + wy) + (ez + wz)
        for j, value in enumerate((ex, wx, ey, wy, ez, wz, d, OMEGA / d)):
            k_ref[j, lo:hi] = value


def whole_sum(level, v_ref, k_ref, emit, first, last):
    xp, xm, y, zplus, zminus = level
    for lo, hi in chunks(first, last):
        ext = v_ref[lo : hi + 2]
        v = ext[1:-1]
        up, down = y(ext)
        k = [k_ref[j, lo:hi] for j in range(6)]
        s = (k[0] * xp(v) + k[1] * xm(v)) + (k[2] * up + k[3] * down)
        emit(lo, hi, v, s + (k[4] * zplus(v) + k[5] * zminus(v)))


def whole_sweep(level, v_ref, to_ref, b_ref, k_ref, first=0, last=GY):
    def emit(lo, hi, v, s):
        to_ref[lo + 1 : hi + 1] = (1.0 - OMEGA) * v + k_ref[7, lo:hi] * (b_ref[lo + 1 : hi + 1] + s)

    whole_sum(level, v_ref, k_ref, emit, first, last)
    if last - first == GY:
        wrap_rows(to_ref)


def coarsen_lanes(v):
    s = v + pltpu.roll(v, 64, 2)
    s = s + pltpu.roll(s, 32, 2)
    return s + jnp.where(lane(v.shape) % 2 == 0, pltpu.roll(s, 127, 2), pltpu.roll(s, 1, 2))


def kernel(
    src_ref, cond_ref, guess_ref, out_ref,
    V0, B0, C0, CX0, CY0, CZ0, W0, VA0, VB0, VH, TR, PE0, TP0,
    C1, CX1, CY1, CZ1, W1, B1, VA1, VB1, R1, TP1,
    C2, CX2, CY2, CZ2, W2, B2, VA2, VB2, R2, B2H, V2H,
    C3, B3, V3A, V3B, K3, C4, B4, V4A, V4B, K4, GC, GB,
    MR, M3, MP1, MP3, ROWS,
    lsem, e0s, e0r, c1s, c1r, b1s, b1r, h0s, h0r, h2s, h2r, cg, bg,
):
    gx, gy = lax.axis_index("gx"), lax.axis_index("gy")
    yc, zc = lax.rem(gy, NYC), lax.div(gy, NYC)

    def beside(dx, dy):
        return (lax.rem(gx + dx + GX, GX), lax.rem(gy + dy + GY, GY))

    def along_z(k):
        return (gx, lax.rem(zc + k, NZC) * NYC + yc)

    def remote(src, dst, send, recv, device):
        return pltpu.make_async_remote_copy(
            src_ref=src, dst_ref=dst, send_sem=send, recv_sem=recv, device_id=device, device_id_type=MESH
        )

    loads = []
    for i, (ref, to) in enumerate(((cond_ref, C0), (guess_ref, V0), (src_ref, B0))):
        for h in range(2):
            loads.append(
                pltpu.make_async_copy(
                    ref.at[:, :, pl.ds(128 * h, 128)],
                    to.at[pl.ds(3, 16), h, pl.ds(4, 16), :],
                    lsem.at[2 * i + h],
                )
            )
    barrier = pltpu.get_barrier_semaphore()
    for dx, dy in EIGHT:
        pl.semaphore_signal(barrier, inc=1, device_id=beside(dx, dy), device_id_type=MESH)

    columns = [lax.rem(gx + d, GX) for d in range(GX)]
    rows = [zc * NYC + lax.rem(yc + d, NYC) for d in range(NYC)]
    for dx, dy in FAR_FIRST:
        pl.semaphore_signal(barrier, inc=1, device_id=(columns[dx], rows[dy]), device_id_type=MESH)
    for k in Z_FAR_FIRST:
        pl.semaphore_signal(barrier, inc=1, device_id=along_z(k), device_id_type=MESH)
    for copy in loads:
        copy.start()

    pl.semaphore_wait(barrier, len(EIGHT) + GX * NYC - 1 + NZC - 1)

    def edge(base, extent, step, width):
        if step == 0:
            return base, base, extent
        if step == 1:
            return base + extent - width, base - width, width
        return base, base + extent, width

    def block_copy(ref, base, extent, step, width, send, recv):
        sx, tx, nx = edge(base[0], extent, step[0], width)
        sy, ty, ny = edge(base[1], extent, step[1], width)
        if len(ref.shape) == 4:
            src, dst = ref.at[pl.ds(sx, nx), :, pl.ds(sy, ny), :], ref.at[pl.ds(tx, nx), :, pl.ds(ty, ny), :]
        else:
            src, dst = ref.at[pl.ds(sx, nx), pl.ds(sy, ny), :], ref.at[pl.ds(tx, nx), pl.ds(ty, ny), :]
        return remote(src, dst, send, recv, beside(*step))

    def exchange(ref, base, extent, width, send, recv, corner=None):
        return [
            block_copy(ref, base, extent, o, corner if corner and o[0] and o[1] else width, send.at[i], recv.at[i])
            for i, o in enumerate(EIGHT)
        ]

    e0c = exchange(C0, (3, 4), 16, 3, e0s.at[0], e0r.at[0], 2)
    e0v = exchange(V0, (3, 4), 16, 3, e0s.at[1], e0r.at[1], 2)
    e0b = exchange(B0, (3, 4), 16, 2, e0s.at[2], e0r.at[2], 1)
    for first in (0, 4, 6):
        for n, copies in enumerate((e0c, e0v, e0b)):
            if first == 0:
                loads[2 * n].wait()
                loads[2 * n + 1].wait()
            for copy in copies[first : first + 4 if first == 0 else first + 2]:
                copy.start()

    def matrix(rows, columns, rule):
        r = lax.broadcasted_iota(jnp.int32, (2 * rows, columns), 0) % rows
        c = lax.broadcasted_iota(jnp.int32, (2 * rows, columns), 1)
        return jnp.where(rule(r, c), 1.0, 0.0).astype(BF16)

    MR[...] = matrix(256, 128, lambda r, c: r // 2 == c)
    M3[...] = matrix(128, 128, lambda r, c: (r % 2 == 0) & (r // 4 == c % 32))
    MP1[...] = matrix(128, 256, lambda r, c: r == c // 2)
    MP3[...] = matrix(128, 512, lambda r, c: (r // 32 == c // 128) & (r % 32 == (c % 128) // 4))

    def restrict_zero(ref, scale):
        pairs = [
            jnp.concatenate([ref[3 + 2 * k, h, 4:20] + ref[4 + 2 * k, h, 4:20] for h in range(2)], axis=1)
            for k in range(8)
        ]
        TR[0:8, 0:16] = mm(jnp.concatenate(pairs, axis=0), MR[...]).reshape(8, 16, 128)
        return (TR[0:8, pl.ds(0, 8, stride=2), :] + TR[0:8, pl.ds(1, 8, stride=2), :]) * scale

    def restrict_one(ref, x0, count, y0, rows, scale):
        for k in range(count):
            TR[k, 0:rows] = ref[x0 + 2 * k, y0 : y0 + rows] + ref[x0 + 1 + 2 * k, y0 : y0 + rows]
        half = rows // 2
        s = (TR[0:count, pl.ds(0, half, stride=2), :] + TR[0:count, pl.ds(1, half, stride=2), :]) * scale
        return s + jnp.where(lane(s.shape) % 2 == 0, pltpu.roll(s, 127, 2), pltpu.roll(s, 1, 2))

    def restrict_two(ref, scale):
        pairs = jnp.concatenate([ref[4] + ref[5], ref[6] + ref[7]], axis=0)
        s = mm(pairs, M3[...]) * scale
        group = lax.broadcasted_iota(jnp.int32, (1, 128), 1) // 32
        row = jnp.zeros((1, 128), F32)
        for g in range(4):
            at = 16 * (g // 2) + 4 + 2 * (g % 2)
            row = jnp.where(group == g, s[at : at + 1] + s[at + 1 : at + 2], row)
        return row

    def z_copy(ref, k, sems):
        src = ref.at[NZC // 2, yc, pl.ds(gx, 1), :]
        dst = ref.at[(NZC // 2 - k) % NZC, yc, pl.ds(gx, 1), :]
        return remote(src, dst, sems.at[0], sems.at[1], along_z(k))

    def plane_copy(ref, dx, dy, sems):
        part = ref.at[:, yc, pl.ds(gx, 1), :]
        return remote(part, part, sems.at[2], sems.at[3], (columns[dx], rows[dy]))

    def start_z(ref, sems):
        for k in Z_FAR_FIRST:
            z_copy(ref, k, sems).start()

    def start_plane(ref, sems):
        for dx, dy in FAR_FIRST:
            plane_copy(ref, dx, dy, sems).start()

    def all_bytes(kind, sem):
        part = ROWS.at[0, pl.ds(0, NZC - 1), :] if kind == 0 else ROWS
        pltpu.make_async_copy(part, part, sem).wait()

    def landed_z(sems):
        all_bytes(0, sems.at[1])

    def landed_plane(sems):
        all_bytes(1, sems.at[3])

    def sent(sems):
        all_bytes(0, sems.at[0])
        all_bytes(1, sems.at[2])

    C1[8:16, 8:16] = restrict_zero(C0, 0.125 * 0.25)
    c1 = exchange(C1, (8, 8), 8, 8, c1s, c1r)
    C2[4:8, 4:8] = restrict_one(C1, 8, 4, 8, 8, 0.125 * 0.25)
    GC[NZC // 2, yc, pl.ds(gx, 1), :] = restrict_two(C2, 0.125 * 0.25)
    start_z(GC, cg)

    for copy in e0c:
        copy.wait_recv()
    for copy in c1:
        copy.start()
    coefficients(C0, CX0, CY0, CZ0, W0, 22)
    for copy in e0v + e0b:
        copy.wait_recv()
    zero = (B0, CX0, CY0, CZ0)
    sweep(V0, VA0, *zero, W0, 1, 21)
    sweep(VA0, VB0, *zero, W0, 2, 20)
    flux_loop(VB0, *zero, 3, 19, lambda x, v, r: put(VA0, x, r))
    B1[8:16, 8:16] = restrict_zero(VA0, 0.125)
    b1 = exchange(B1, (8, 8), 8, 6, b1s, b1r, 5)
    for copy in b1:
        copy.start()

    h0 = [
        remote(VB0.at[pl.ds(sx, nx), :, pl.ds(sy, ny), :], VH.at[pl.ds(tx, nx), :, pl.ds(ty, ny), :],
               h0s.at[i], h0r.at[i], beside(*o))
        for i, (o, (sx, tx, nx), (sy, ty, ny)) in enumerate((
            ((0, 1), (3, 3, 16), (18, 2, 1)),
            ((0, -1), (3, 3, 16), (5, 21, 1)),
            ((1, 0), (17, 1, 1), (4, 4, 16)),
            ((-1, 0), (4, 20, 1), (4, 4, 16)),
            ((1, 1), (18, 2, 1), (19, 3, 1)),
            ((1, -1), (18, 2, 1), (4, 20, 1)),
            ((-1, 1), (3, 19, 1), (19, 3, 1)),
            ((-1, -1), (3, 19, 1), (4, 20, 1)),
        ))
    ]
    for copy in h0:
        copy.start()

    landed_z(cg)
    start_plane(GC, cg)

    for copy in c1:
        copy.wait_recv()
    coefficients(C1, CX1, CY1, CZ1, W1, 24)
    for k in range(3):
        C2[4 * k : 4 * k + 4, 0:12] = restrict_one(C1, 8 * k, 4, 0, 24, 0.125 * 0.25)
    coefficients(C2, CX2, CY2, CZ2, W2, 12)

    for copy in b1:
        copy.wait_recv()

    def from_zero(to_ref, b_ref, w_ref, lo, hi):
        to_ref[lo:hi] = w_ref[lo:hi] * b_ref[lo:hi]

    one = (B1, CX1, CY1, CZ1)
    from_zero(VA1, B1, W1, 2, 22)
    sweep(VA1, VB1, *one, W1, 3, 21)
    flux_loop(VB1, *one, 4, 20, lambda x, v, r: put(R1, x, r))
    B2[2:10, 0:12] = restrict_one(R1, 4, 8, 0, 24, 0.125)

    two = (B2, CX2, CY2, CZ2)
    from_zero(VA2, B2, W2, 2, 10)
    sweep(VA2, VB2, *two, W2, 3, 9)
    flux_loop(VB2, *two, 4, 8, lambda x, v, r: put(R2, x, r))
    GB[NZC // 2, yc, pl.ds(gx, 1), :] = restrict_two(R2, 0.125)
    start_z(GB, bg)
    B2H[4:8, 4:8] = B2[4:8, 4:8]
    V2H[4:8, 4:8] = VB2[4:8, 4:8]
    h2 = exchange(B2H, (4, 4), 4, 4, h2s.at[0], h2r.at[0]) + exchange(V2H, (4, 4), 4, 4, h2s.at[1], h2r.at[1])
    for copy in h2:
        copy.start()

    landed_z(bg)
    start_plane(GB, bg)
    landed_plane(cg)
    C3[1 : GY + 1] = GC[...].reshape(GY, GX, 128)
    wrap_rows(C3)
    whole_coefficients(THREE, C3, K3)
    C4[1 : GY + 1] = coarsen_lanes(C3[1 : GY + 1]) * (0.125 * 0.25)
    wrap_rows(C4)
    whole_coefficients(FOUR, C4, K4)

    landed_plane(bg)

    b3 = GB[...].reshape(GY, GX, 128)
    mean = jnp.sum(jnp.sum(b3, axis=0), keepdims=True) * (1.0 / (GY * GX * 128))
    B3[1 : GY + 1] = b3
    V3A[1 : GY + 1] = K3[7] * b3
    wrap_rows(V3A)
    whole_sweep(THREE, V3A, V3B, B3, K3, 5, 31)

    def residual(lo, hi, v, s):
        r = B3[lo + 1 : hi + 1] + s - K3[6, lo:hi] * v
        B4[lo + 1 : hi + 1] = coarsen_lanes(r) * 0.125

    whole_sum(THREE, V3B, K3, residual, 6, 30)

    b4 = B4[7:31] - mean
    B4[7:31] = b4
    V4A[7:31] = K4[7, 6:30] * b4
    here, there = V4A, V4B
    for i in range(7):
        whole_sweep(FOUR, here, there, B4, K4, 7 + i, 29 - i)
        here, there = there, here

    V3B[14:24] = V3B[14:24] + here[14:24]
    whole_sweep(THREE, V3B, V3A, B3, K3, 14, 22)
    whole_sweep(THREE, V3A, V3B, B3, K3, 15, 21)

    near = [
        pltpu.roll(V3B[4 * (NZC // 2) + yc + j], lax.rem(1 - gx + GX, GX), 0) for j in range(3)
    ]
    u = mm(jnp.concatenate(near, axis=0), MP3[...])
    for copy in h2:
        copy.wait_recv()
    pair = lax.broadcasted_iota(jnp.int32, (16, 128), 0) // 2
    for x3 in range(6):
        i, dx = x3 // 2, x3 % 2
        rise = jnp.zeros((16, 128), F32)
        for y3 in range(6):
            j, g = y3 // 2, 2 * dx + y3 % 2
            rise = jnp.where(pair == y3, u[8 * j + i : 8 * j + i + 1, 128 * g : 128 * g + 128], rise)
        for x in (2 * x3, 2 * x3 + 1):
            VA2[x] = V2H[x] + rise
    two = (B2H, CX2, CY2, CZ2)
    sweep(VA2, R2, *two, W2, 1, 11)
    sweep(R2, VA2, *two, W2, 2, 10)

    for k in range(8):
        cells = VA2[2 + k, 0:12, :]
        TP1[k, pl.ds(0, 12, stride=2), :] = cells
        TP1[k, pl.ds(1, 12, stride=2), :] = cells
    for x in range(5, 19):
        VA1[x] = VB1[x] + TP1[x // 2 - 2]
    sweep(VA1, R1, *one, W1, 6, 18)
    sweep(R1, VA1, *one, W1, 7, 17)

    for k in range(10):
        cells = VA1[7 + k, 7:17, :]
        TP0[k, pl.ds(2, 10, stride=2), :] = cells
        TP0[k, pl.ds(3, 10, stride=2), :] = cells
    u = mm(TP0[...].reshape(10 * 24, 128), MP1[...])
    for h in range(2):
        PE0[:, h] = u[:, 128 * h : 128 * h + 128].reshape(10, 24, 128)
    for copy in h0:
        copy.wait_recv()
    row = lax.broadcasted_iota(jnp.int32, (24, 128), 0)
    outer = (row == 2) | (row == 21)

    def raise_slab(x, carry):
        for h in range(2):
            VA0[x, h] = jnp.where(outer, VH[x, h], VB0[x, h]) + PE0[lax.div(x - 1, 2), h]
        return carry

    lax.fori_loop(3, 19, raise_slab, 0, unroll=8)
    corner = (row == 3) | (row == 20)
    for h in range(2):
        for x in (1, 20):
            VA0[x, h] = VH[x, h] + PE0[(x - 1) // 2, h]
        for x in (2, 19):
            VA0[x, h] = jnp.where(corner, VH[x, h], VB0[x, h]) + PE0[(x - 1) // 2, h]
    for copy in e0c + e0v + e0b:
        copy.wait_send()
    sweep(VA0, V0, *zero, W0, 2, 20)

    def last(x, v, r):
        s = add(v, mul(get(W0, x), r))
        for h in range(2):
            out_ref[x - 3, :, 128 * h : 128 * h + 128] = s[h][4:20]

    flux_loop(V0, *zero, 3, 19, last)

    for copy in c1 + b1 + h0 + h2:
        copy.wait_send()
    sent(cg)
    sent(bg)


def solution(mesh):
    def vmem(*shape):
        return pltpu.VMEM(shape, F32)

    def half(*shape):
        return pltpu.VMEM(shape, BF16)

    dma = pltpu.SemaphoreType.DMA
    scratch = (
        [vmem(22, 2, 24, 128)] * 10
        + [vmem(8, 24, 128), vmem(10, 2, 24, 128), vmem(10, 24, 128)]
        + [vmem(24, 24, 128)] * 9
        + [vmem(8, 24, 128)]
        + [vmem(12, 16, 128)] * 11
        + [vmem(GY + 2, GX, 128)] * 4
        + [vmem(8, GY, GX, 128)]
        + [vmem(GY + 2, GX, 128)] * 4
        + [vmem(8, GY, GX, 128)]
        + [vmem(NZC, NYC, GX, 128)] * 2
        + [half(512, 128), half(256, 128), half(256, 256), half(256, 512)]
        + [vmem(GX * NYC - 1, NZC, 128)]
        + [dma((6,)), dma((3, 8)), dma((3, 8))]
        + [dma((8,))] * 6
        + [dma((2, 8))] * 2
        + [dma((4,))] * 2
    )

    def step(source, conductivity, guess):
        return pl.pallas_call(
            kernel,
            out_shape=jax.ShapeDtypeStruct(source.shape, F32),
            in_specs=[pl.BlockSpec(memory_space=pl.ANY)] * 3,
            out_specs=pl.BlockSpec(memory_space=pltpu.VMEM),
            scratch_shapes=scratch,
            compiler_params=pltpu.CompilerParams(
                collective_id=0, has_side_effects=True, vmem_limit_bytes=54848 * 2**10
            ),
            name="vcycle",
        )(source, conductivity, guess)

    spec = P("gx", "gy", None)
    return jax.shard_map(step, mesh=mesh, in_specs=(spec, spec, spec), out_specs=spec, check_vma=False)
```
